256 devices in a mesh: dp: 32 (over x, y, core), tensor: 8 (over z).
Axes of the slice: x: 4, y: 4, z: 8, core: 2. Of those that a mesh axis runs over, the one named last changes fastest.
Arguments:
- grads: bfloat16 [2, 32, 8192, 512], P(None, 'dp', 'tensor'), may hold values from -48 to 48
- errors: float32 [2, 32, 8192, 512], P(None, 'dp', 'tensor'), may hold values from -6 to 6
- q_prev: float32 [2, 512, 32], replicated, may hold values from -6 to 6
Outputs:
- decompressed: bfloat16 [2, 8192, 512], P(None, 'tensor')
- new_errors: float32 [2, 32, 8192, 512], P(None, 'dp', 'tensor')
- q_new: float32 [2, 512, 32], replicated
The draws below stay inside these ranges and needn't reach their ends.
All inputs are finite; a program needn't handle non-finite values.
Results may differ from the reference program's by a relative error of at most 0.001.
Values sent between devices are 32-bit elements; how exact they have to be, the bound alone decides.
No kernel may reach another device: no remote copies, remote signals or barrier semaphores. Data moves between devices by JAX's collectives and lax.ppermute only.
A program may use at most 64 MiB of HBM per device.

```python
import jax
import jax.numpy as jnp
from jax import lax

LAYERS = 2
D = 8192
COLS = 512
RANK = 32
REPLICAS = 32


def draw_grads(key, part):
    key = jax.random.fold_in(key, 11)
    key_shared, key_own = jax.random.split(key, 2)
    shared = jax.random.normal(key_shared, (LAYERS, 1, D, COLS), jnp.float32) * 4.0
    own = jax.random.normal(key_own, (LAYERS, REPLICAS, D, COLS), jnp.float32)
    return jnp.clip(shared + own, -48.0, 48.0).astype(jnp.bfloat16)


def shard_levels(key, dims, cuts, least, high):
    level, own = 1.0, jax.random.fold_in(key, 6)
    for axis_at, parts in cuts:
        draws = jnp.exp(jax.random.uniform(jax.random.fold_in(own, axis_at), (parts,), jnp.float32, least / len(cuts), high / len(cuts)))
        level = level * jnp.repeat(draws, dims[axis_at] // parts).reshape([-1 if axis == axis_at else 1 for axis in range(len(dims))])
    return level


def bell_draw(key, shape, deviation, limit, cuts=(), dtype=jnp.bfloat16):
    result = jax.random.normal(key, shape, jnp.float32) * deviation
    if len(cuts) > 0:
        result = shard_levels(key, shape, cuts, -0.22, 0.18) * result
    return jnp.clip(result, min=-limit, max=limit).astype(dtype)


def setup_inputs(seed: int = 0) -> dict:
    key_of = jax.random.split(jax.random.key(seed), 4)
    return {
        "grads": draw_grads(jax.random.fold_in(key_of[3], 71), 0),
        "errors": bell_draw(key_of[1], (LAYERS, REPLICAS, D, COLS), 1.0, 6.0, ((1, 32), (2, 8)), jnp.float32),
        "q_prev": bell_draw(key_of[2], (LAYERS, COLS, RANK), 1.0, 6.0, (), jnp.float32),
    }


def reference(grads, errors, q_prev):
    highest = lax.Precision.HIGHEST
    outs_dec = []
    outs_err = []
    outs_q = []
    for layer in range(LAYERS):
        grad_layer = grads[layer]
        error_layer = errors[layer]
        warm = q_prev[layer]

        def left_step(total, pair):
            merged = pair[0].astype(jnp.float32) + pair[1]
            return (total + jnp.dot(merged, warm, precision=highest), None)
        factor, _ = lax.scan(left_step, jnp.zeros((D, RANK), jnp.float32), (grad_layer, error_layer))
        factor = factor / REPLICAS
        gram = jnp.dot(factor.T, factor, precision=highest)
        lower = jnp.linalg.cholesky(gram)
        p_hat = lax.linalg.triangular_solve(lower, factor, left_side=False, lower=True, transpose_a=True)

        def right_step(total, pair):
            merged = pair[0].astype(jnp.float32) + pair[1]
            return (total + jnp.dot(merged.T, p_hat, precision=highest), None)
        right, _ = lax.scan(right_step, jnp.zeros((COLS, RANK), jnp.float32), (grad_layer, error_layer))
        right = right / REPLICAS
        approx = jnp.dot(p_hat, right.T, precision=highest)
        outs_dec.append(approx.astype(jnp.bfloat16))
        outs_err.append(grad_layer.astype(jnp.float32) + error_layer - approx[None])
        outs_q.append(right)
    return (jnp.stack(outs_dec), jnp.stack(outs_err), jnp.stack(outs_q))
```

```python
import jax
import jax.numpy as jnp
from jax import lax
from jax.experimental import pallas as pl
from jax.experimental.pallas import tpu as pltpu
from jax.sharding import PartitionSpec as P

highest = lax.Precision.HIGHEST
f32, bf16 = jnp.float32, jnp.bfloat16
block_rows = 256


def halves(x):
    high = x.astype(bf16)
    return high, (x - high.astype(f32)).astype(bf16)


def thirds(x):
    high = x.astype(bf16)
    rest = x - high.astype(f32)
    return high, *halves(rest)


def dot(a, b, contract, precision=None):
    return lax.dot_general(a, b, (contract, ((), ())), precision=precision, preferred_element_type=f32)


def split_dot(small, high, low, contract):
    rows = small.shape[0]
    one, two, three = thirds(small)
    by_high = dot(jnp.concatenate([one, two, three], 0), high, contract)
    by_low = dot(jnp.concatenate([one, two], 0), low, contract)
    small_terms = by_high[rows : 2 * rows] + by_low[:rows]
    tiny_terms = by_high[2 * rows :] + by_low[rows:]
    return by_high[:rows] + (small_terms + tiny_terms)


def left_kernel(grads, errors, q_t, high, low, part):
    merged = grads[0].astype(f32) + errors[0]
    merged_high, merged_low = halves(merged)
    high[0] = merged_high
    low[0] = merged_low
    term = split_dot(q_t[0], merged_high, merged_low, ((1,), (1,)))
    for at in range(part.shape[1]):
        part[0, at] = term[:, at * 128 : (at + 1) * 128]


def left(grads, errors, q_t):
    layers, rows, cols = grads.shape
    rank = q_t.shape[1]
    lanes = block_rows // 128
    wide = pl.BlockSpec((1, block_rows, cols), lambda l, b: (l, b, 0))
    return pl.pallas_call(
        left_kernel,
        grid=(layers, rows // block_rows),
        in_specs=[wide, wide, pl.BlockSpec((1, rank, cols), lambda l, b: (l, 0, 0))],
        out_specs=[wide, wide, pl.BlockSpec((1, lanes, rank, 128), lambda l, b: (l, b, 0, 0))],
        out_shape=[
            jax.ShapeDtypeStruct(grads.shape, bf16),
            jax.ShapeDtypeStruct(grads.shape, bf16),
            jax.ShapeDtypeStruct((layers, rows // 128, rank, 128), f32),
        ],
        name="left",
    )(grads, errors, q_t)


def spread(x, scale):
    def kernel(x, out):
        total = jnp.sum(x[...], axis=0) * scale
        out[...] = jnp.broadcast_to(total[None], out.shape)

    return pl.pallas_call(kernel, out_shape=jax.ShapeDtypeStruct(x.shape, f32), name="spread")(x)


def right_kernel(high, low, p_t, raw, gram):
    rank = p_t.shape[2]
    factor = jnp.concatenate([p_t[0, at] for at in range(p_t.shape[1])], 1)
    term = split_dot(factor, high[0], low[0], ((1,), (0,)))
    square = dot(factor, factor, ((1,), (1,)), highest)
    packed = jnp.concatenate([square[at : at + 8] for at in range(0, rank, 8)], 1)

    @pl.when(pl.program_id(1) == 0)
    def _():
        for at in range(raw.shape[1]):
            raw[0, at] = term[:, at * 128 : (at + 1) * 128]
        gram[0] = packed

    @pl.when(pl.program_id(1) != 0)
    def _():
        for at in range(raw.shape[1]):
            raw[0, at] += term[:, at * 128 : (at + 1) * 128]
        gram[0] += packed


def right(high, low, p_t):
    layers, rows, cols = high.shape
    rank = p_t.shape[2]
    lanes = block_rows // 128
    wide = pl.BlockSpec((1, block_rows, cols), lambda l, b: (l, b, 0))
    return pl.pallas_call(
        right_kernel,
        grid=(layers, rows // block_rows),
        in_specs=[wide, wide, pl.BlockSpec((1, lanes, rank, 128), lambda l, b: (l, b, 0, 0))],
        out_specs=[
            pl.BlockSpec((1, cols // 128, rank, 128), lambda l, b: (l, 0, 0, 0)),
            pl.BlockSpec((1, 8, 128), lambda l, b: (l, 0, 0)),
        ],
        out_shape=[
            jax.ShapeDtypeStruct((layers, cols // 128, rank, 128), f32),
            jax.ShapeDtypeStruct((layers, 8, 128), f32),
        ],
        name="right",
    )(high, low, p_t)


def mix(raw, gram, copies):
    def kernel(raw, gram, out):
        total = jnp.sum(raw[...], axis=0)
        both = jnp.concatenate([total, gram[0], gram[1]], 0)
        out[...] = jnp.broadcast_to(both[None], out.shape)

    shape = (copies, raw.shape[1] + 16, 128)
    return pl.pallas_call(kernel, out_shape=jax.ShapeDtypeStruct(shape, f32), name="mix")(raw, gram)


def unmix(x, copies, scale):
    def kernel(x, piece, gram):
        total = jnp.sum(x[...], axis=0)
        piece[...] = jnp.broadcast_to(total[None, :8] * scale, piece.shape)
        gram[0] = total[8:16]
        gram[1] = total[16:24]

    return pl.pallas_call(
        kernel,
        out_shape=[jax.ShapeDtypeStruct((copies, 8, 128), f32), jax.ShapeDtypeStruct((2, 8, 128), f32)],
        name="unmix",
    )(x)


def orthonormal_kernel(gram, p_t, inverse, p_hat):
    layers, _, rank, _ = p_t.shape
    squares = [jnp.concatenate([gram[l][:, at : at + rank] for at in range(0, 128, rank)], 0) for l in range(layers)]
    row = lax.broadcasted_iota(jnp.int32, (rank, 128), 0)
    lane = lax.broadcasted_iota(jnp.int32, (rank, 128), 1)
    first = (lane // rank) % 2 == 0
    unit = (lane % rank == row).astype(f32)
    both = jnp.concatenate(squares + [unit[:, : 2 * rank]], 1)
    pivots = jnp.ones((rank, 128), f32)
    for k in range(rank):
        column = jnp.where(first, both[:, k : k + 1], both[:, rank + k : rank + k + 1])
        pivot = column[k : k + 1]
        pivots = jnp.where(row == k, pivot, pivots)
        if k < rank - 1:
            factor = jnp.where(row > k, column / pivot, 0.0)
            both = both - factor * both[k : k + 1]
    scaled = both / jnp.sqrt(pivots)
    for l in range(layers):
        lower_inverse = scaled[:, (2 + l) * rank : (3 + l) * rank]
        inverse[l] = lower_inverse
        for at in range(p_t.shape[1]):
            hat_t = dot(lower_inverse, p_t[l, at], ((1,), (0,)), highest)
            high = hat_t.astype(bf16).astype(f32)
            low = hat_t - high
            stack = jnp.concatenate([high, low, high, jnp.zeros_like(high)], 0)
            p_hat[l, at * 128 : (at + 1) * 128] = stack.T.astype(bf16)


def orthonormal(gram, p_t):
    layers, tiles, rank, _ = p_t.shape
    return pl.pallas_call(
        orthonormal_kernel,
        out_shape=[
            jax.ShapeDtypeStruct((layers, rank, rank), f32),
            jax.ShapeDtypeStruct((layers, tiles * 128, 4 * rank), bf16),
        ],
        cost_estimate=pl.CostEstimate(flops=400_000_000, bytes_accessed=1_000_000, transcendentals=0),
        name="orthonormal",
    )(gram, p_t)


def last_kernel(high, low, p_hat, inverse, raw, decompressed, new_errors, q_new, stack):
    @pl.when(pl.program_id(1) == 0)
    def _():
        whole = jnp.concatenate([raw[0, at] for at in range(raw.shape[1])], 1)
        q = dot(inverse[0], whole, ((1,), (0,)), highest)
        q_new[0] = q
        q_high, q_low = halves(q)
        stack[...] = jnp.concatenate([q_high, q_high, q_low, jnp.zeros_like(q_high)], 0)

    approx = dot(p_hat[0], stack[...], ((1,), (0,)))
    decompressed[0] = approx.astype(bf16)
    new_errors[0] = (high[0].astype(f32) + low[0].astype(f32)) - approx


def last(high, low, p_hat, inverse, raw):
    layers, rows, cols = high.shape
    rank = inverse.shape[1]
    wide = pl.BlockSpec((1, block_rows, cols), lambda l, b: (l, b, 0))
    return pl.pallas_call(
        last_kernel,
        grid=(layers, rows // block_rows),
        in_specs=[
            wide,
            wide,
            pl.BlockSpec((1, block_rows, 4 * rank), lambda l, b: (l, b, 0)),
            pl.BlockSpec((1, rank, rank), lambda l, b: (l, 0, 0)),
            pl.BlockSpec((1, cols // 128, rank, 128), lambda l, b: (l, 0, 0, 0)),
        ],
        out_specs=[wide, wide, pl.BlockSpec((1, rank, cols), lambda l, b: (l, 0, 0))],
        out_shape=[
            jax.ShapeDtypeStruct(high.shape, bf16),
            jax.ShapeDtypeStruct(high.shape, f32),
            jax.ShapeDtypeStruct((layers, rank, cols), f32),
        ],
        scratch_shapes=[pltpu.VMEM((4 * rank, cols), bf16)],
        name="last",
    )(high, low, p_hat, inverse, raw)


def exchange(x, axis):
    return lax.all_to_all(x, axis, 0, 0, tiled=True)


def on_device(grads, errors, q_prev):
    replicas, slabs = lax.axis_size("dp"), lax.axis_size("tensor")
    high, low, part = left(grads[:, 0], errors[:, 0], jnp.swapaxes(q_prev, 1, 2))
    tiles_shape = part.shape
    part = exchange(part.reshape(replicas, -1, 128), "dp")
    p_t = exchange(spread(part, 1.0 / replicas), "dp").reshape(tiles_shape)
    raw, gram = right(high, low, p_t)
    raw_shape = raw.shape
    raw = exchange(raw.reshape(replicas, -1, 128), "dp")
    both = exchange(mix(raw, gram, slabs), "tensor")
    raw, gram = unmix(both, replicas, 1.0 / replicas)
    raw = exchange(raw, "dp").reshape(raw_shape)
    inverse, p_hat = orthonormal(gram, p_t)
    decompressed, new_errors, q_new = last(high, low, p_hat, inverse, raw)
    return decompressed, new_errors[:, None], jnp.swapaxes(q_new, 1, 2)


def solution(mesh):
    placed = (P(None, "dp", "tensor", None), P(None, "dp", "tensor", None), P())
    return jax.shard_map(
        on_device,
        mesh=mesh,
        in_specs=placed,
        out_specs=(P(None, "tensor", None), P(None, "dp", "tensor", None), P()),
        check_vma=False,
    )
```

```python
import jax
import jax.numpy as jnp
from jax import lax
from jax.experimental import pallas as pl
from jax.experimental.pallas import tpu as pltpu
from jax.sharding import PartitionSpec as P

highest = lax.Precision.HIGHEST
f32, bf16 = jnp.float32, jnp.bfloat16
block_rows = 512
ahead = 3


def halves(x):
    high = x.astype(bf16)
    return high, (x - high.astype(f32)).astype(bf16)


def thirds(x):
    high = x.astype(bf16)
    rest = x - high.astype(f32)
    return high, *halves(rest)


def dot(a, b, contract, precision=None):
    return lax.dot_general(a, b, (contract, ((), ())), precision=precision, preferred_element_type=f32)


def split_dot(small, high, low, contract):
    one, two, three = small
    rows = one.shape[0]
    by_high = dot(jnp.concatenate([one, two, three], 0), high, contract)
    by_low = dot(jnp.concatenate([one, two], 0), low, contract)
    small_terms = by_high[rows : 2 * rows] + by_low[:rows]
    tiny_terms = by_high[2 * rows :] + by_low[rows:]
    return by_high[:rows] + (small_terms + tiny_terms)


def in_vmem(x):
    return pltpu.with_memory_space_constraint(x, pltpu.VMEM)


whole = pl.BlockSpec(memory_space=pltpu.VMEM)
params = pltpu.CompilerParams(vmem_limit_bytes=16 * 1024 * 1024)


def in_hbm(x):
    return pltpu.with_memory_space_constraint(x, pltpu.HBM)


def left_kernel(grads, errors, q_t, terms, part, grads_here, errors_here, q_here, q_sem, grads_sem, errors_sem):
    layers, _, rows, _ = terms.shape
    pieces = [(l, b) for l in range(layers) for b in range(rows // block_rows)]

    def fetch(n):
        l, b = pieces[n]
        at = pl.ds(b * block_rows, block_rows)
        return (
            pltpu.make_async_copy(grads.at[l, at], grads_here.at[l, at], grads_sem.at[n]),
            pltpu.make_async_copy(errors.at[l, at], errors_here.at[l, at], errors_sem.at[n]),
        )

    q_copy = pltpu.make_async_copy(q_t, q_here, q_sem)
    q_copy.start()
    for n in range(ahead):
        for copy in fetch(n):
            copy.start()
    q_copy.wait()
    for n, (l, b) in enumerate(pieces):
        for copy in fetch(n):
            copy.wait()
        if n + ahead < len(pieces):
            for copy in fetch(n + ahead):
                copy.start()
        at = pl.ds(b * block_rows, block_rows)
        merged = grads_here[l, at].astype(f32) + errors_here[l, at]
        merged_high, merged_low = halves(merged)
        terms[l, 0, at] = merged_high
        terms[l, 1, at] = merged_low
        term = split_dot(thirds(q_here[l]), merged_high, merged_low, ((1,), (1,)))
        for lane in range(block_rows // 128):
            part[l, b * (block_rows // 128) + lane] = term[:, lane * 128 : (lane + 1) * 128]


def left(grads, errors, q_t):
    layers, rows, cols = grads.shape
    rank = q_t.shape[1]
    pieces = layers * rows // block_rows
    return pl.pallas_call(
        left_kernel,
        in_specs=[pl.BlockSpec(memory_space=pltpu.HBM)] * 3,
        out_specs=[whole] * 2,
        out_shape=[
            pltpu.VMEM((layers, 2, rows, cols), bf16),
            pltpu.VMEM((layers, rows // 128, rank, 128), f32),
        ],
        scratch_shapes=[
            pltpu.VMEM(grads.shape, bf16),
            pltpu.VMEM(grads.shape, f32),
            pltpu.VMEM(q_t.shape, f32),
            pltpu.SemaphoreType.DMA,
            pltpu.SemaphoreType.DMA((pieces,)),
            pltpu.SemaphoreType.DMA((pieces,)),
        ],
        compiler_params=params,
        name="left",
    )(in_hbm(grads), in_hbm(errors), in_hbm(q_t))


def spread(x, scale):
    def kernel(x, out):
        total = jnp.sum(x[...], axis=0) * scale
        out[...] = jnp.broadcast_to(total[None], out.shape)

    return pl.pallas_call(
        kernel,
        in_specs=[whole],
        out_specs=whole,
        out_shape=pltpu.VMEM(x.shape, f32),
        compiler_params=params,
        name="spread",
    )(in_vmem(x))


def right_kernel(terms, p_t, raw, gram, p_terms):
    layers, tiles, rank, _ = p_t.shape
    for l in range(layers):
        factor = jnp.concatenate([p_t[l, at] for at in range(tiles)], 1)
        small = thirds(factor)
        term = split_dot(small, terms[l, 0], terms[l, 1], ((1,), (0,)))
        for at in range(raw.shape[1]):
            raw[l, at] = term[:, at * 128 : (at + 1) * 128]
        square = dot(factor, factor, ((1,), (1,)), highest)
        gram[l] = jnp.concatenate([square[at : at + 8] for at in range(0, rank, 8)], 1)
        stack = jnp.concatenate([small[0], small[1], small[0], jnp.zeros_like(small[0])], 0)
        p_terms[l] = stack.T


def right(terms, p_t):
    layers, _, rows, cols = terms.shape
    rank = p_t.shape[2]
    return pl.pallas_call(
        right_kernel,
        in_specs=[whole] * 2,
        out_specs=[whole] * 3,
        out_shape=[
            pltpu.VMEM((layers, cols // 128, rank, 128), f32),
            pltpu.VMEM((layers, 8, 128), f32),
            pltpu.VMEM((layers, rows, 4 * rank), bf16),
        ],
        compiler_params=params,
        name="right",
    )(in_vmem(terms), in_vmem(p_t))


def mix(raw, gram, copies):
    def kernel(raw, gram, out):
        total = jnp.sum(raw[...], axis=0)
        both = jnp.concatenate([total, gram[0], gram[1]], 0)
        out[...] = jnp.broadcast_to(both[None], out.shape)

    return pl.pallas_call(
        kernel,
        in_specs=[whole] * 2,
        out_specs=whole,
        out_shape=pltpu.VMEM((copies, raw.shape[1] + 16, 128), f32),
        compiler_params=params,
        name="mix",
    )(in_vmem(raw), in_vmem(gram))


def lower_inverses(packed, rank):
    groups = rank // 8
    row = lax.broadcasted_iota(jnp.int32, (8, 128), 0)
    lane = lax.broadcasted_iota(jnp.int32, (8, 128), 1)
    first = (lane // rank) % 2 == 0
    tiles = []
    for g in range(groups):
        squares = [tile[:, g * rank : (g + 1) * rank] for tile in packed]
        unit = (lane % rank == row + 8 * g).astype(f32)
        tiles.append(jnp.concatenate(squares + [unit[:, 2 * rank :]], 1))
    pivots = [jnp.ones((8, 128), f32)] * groups
    for start in range(0, rank, 16):
        columns = {}
        for k in range(start, start + 16):
            for g in range(start // 8, groups):
                columns[k, g] = jnp.where(first, tiles[g][:, k : k + 1], tiles[g][:, rank + k : rank + k + 1])
        for k in range(start, start + 16):
            at, s = divmod(k, 8)
            pivot = columns[k, at][s : s + 1]
            pivots[at] = jnp.where(row == s, pivot, pivots[at])
            over = 1.0 / pivot
            pivot_row = tiles[at][s : s + 1] * over
            entries = {j: columns[j, at][s : s + 1] * over for j in range(k + 1, start + 16)}
            for g in range(at, groups):
                column = columns[k, g]
                if g == at:
                    column = jnp.where(row > s, column, 0.0)
                tiles[g] = tiles[g] - column * pivot_row
                for j, entry in entries.items():
                    columns[j, g] = columns[j, g] - column * entry
    both = jnp.concatenate([tile / jnp.sqrt(pivot) for tile, pivot in zip(tiles, pivots)], 0)
    return [both[:, (2 + l) * rank : (3 + l) * rank] for l in range(2)]


def unmix(x, copies, rank, scale):
    def kernel(x, piece, inverse):
        total = jnp.sum(x[...], axis=0)
        piece[...] = jnp.broadcast_to(total[None, :8] * scale, piece.shape)
        inverse[0], inverse[1] = lower_inverses([total[8:16], total[16:24]], rank)

    return pl.pallas_call(
        kernel,
        in_specs=[whole],
        out_specs=[whole] * 2,
        out_shape=[pltpu.VMEM((copies, 8, 128), f32), pltpu.VMEM((2, rank, rank), f32)],
        compiler_params=params,
        name="unmix",
    )(in_vmem(x))


def last_kernel(
    terms, p_terms, inverse, raw, decompressed, new_errors, q_new,
    decompressed_here, errors_here, q_here, decompressed_sem, errors_sem, q_sem,
):
    layers, _, rows, _ = terms.shape
    copies = []

    def send(source, target, sem):
        copy = pltpu.make_async_copy(source, target, sem)
        copy.start()
        copies.append(copy)

    for l in range(layers):
        sums = jnp.concatenate([raw[l, at] for at in range(raw.shape[1])], 1)
        q = dot(inverse[l], sums, ((1,), (0,)), highest)
        q_here[l] = q
        send(q_here.at[l], q_new.at[l], q_sem.at[l])
        right_high, right_low = halves(dot(inverse[l], q, ((0,), (0,)), highest))
        stack = jnp.concatenate([right_high, right_high, right_low, jnp.zeros_like(right_high)], 0)
        for b in range(rows // block_rows):
            at = pl.ds(b * block_rows, block_rows)
            n = l * (rows // block_rows) + b
            approx = dot(p_terms[l, at], stack, ((1,), (0,)))
            decompressed_here[l, at] = approx.astype(bf16)
            errors_here[l, at] = (terms[l, 0, at].astype(f32) + terms[l, 1, at].astype(f32)) - approx
            send(decompressed_here.at[l, at], decompressed.at[l, at], decompressed_sem.at[n])
            send(errors_here.at[l, at], new_errors.at[l, at], errors_sem.at[n])
    for copy in copies:
        copy.wait()


def last(terms, p_terms, inverse, raw):
    layers, _, rows, cols = terms.shape
    shape = (layers, rows, cols)
    rank = inverse.shape[1]
    pieces = layers * rows // block_rows
    return pl.pallas_call(
        last_kernel,
        in_specs=[whole] * 4,
        out_specs=[pl.BlockSpec(memory_space=pltpu.HBM)] * 3,
        out_shape=[
            pltpu.HBM(shape, bf16),
            pltpu.HBM(shape, f32),
            pltpu.HBM((layers, rank, cols), f32),
        ],
        scratch_shapes=[
            pltpu.VMEM(shape, bf16),
            pltpu.VMEM(shape, f32),
            pltpu.VMEM((layers, rank, cols), f32),
            pltpu.SemaphoreType.DMA((pieces,)),
            pltpu.SemaphoreType.DMA((pieces,)),
            pltpu.SemaphoreType.DMA((layers,)),
        ],
        compiler_params=params,
        name="last",
    )(in_vmem(terms), in_vmem(p_terms), in_vmem(inverse), in_vmem(raw))


def exchange(x, axis):
    return lax.all_to_all(x, axis, 0, 0, tiled=True)


def on_device(grads, errors, q_prev):
    replicas, slabs = lax.axis_size("dp"), lax.axis_size("tensor")
    terms, part = left(grads[:, 0], errors[:, 0], jnp.swapaxes(q_prev, 1, 2))
    tiles_shape = part.shape
    part = exchange(part.reshape(replicas, -1, 128), "dp")
    p_t = exchange(spread(part, 1.0 / replicas), "dp").reshape(tiles_shape)
    raw, gram, p_terms = right(terms, p_t)
    raw_shape = raw.shape
    raw = exchange(raw.reshape(replicas, -1, 128), "dp")
    both = exchange(mix(raw, gram, slabs), "tensor")
    raw, inverse = unmix(both, replicas, p_t.shape[2], 1.0 / replicas)
    raw = exchange(raw, "dp").reshape(raw_shape)
    decompressed, new_errors, q_new = last(terms, p_terms, inverse, raw)
    return decompressed, new_errors[:, None], jnp.swapaxes(q_new, 1, 2)


def solution(mesh):
    placed = (P(None, "dp", "tensor", None), P(None, "dp", "tensor", None), P())
    return jax.shard_map(
        on_device,
        mesh=mesh,
        in_specs=placed,
        out_specs=(P(None, "tensor", None), P(None, "dp", "tensor", None), P()),
        check_vma=False,
    )
```

```python
import jax
import jax.numpy as jnp
from jax import lax
from jax.experimental import pallas as pl
from jax.experimental.pallas import tpu as pltpu
from jax.sharding import PartitionSpec as P

highest = lax.Precision.HIGHEST
f32, bf16 = jnp.float32, jnp.bfloat16
block_rows = 512
ahead = 3


def halves(x):
    high = x.astype(bf16)
    return high, (x - high.astype(f32)).astype(bf16)


def thirds(x):
    high = x.astype(bf16)
    rest = x - high.astype(f32)
    return high, *halves(rest)


def dot(a, b, contract, precision=None):
    return lax.dot_general(a, b, (contract, ((), ())), precision=precision, preferred_element_type=f32)


def split_dot(small, high, low, contract):
    one, two, three = small
    rows = one.shape[0]
    by_high = dot(jnp.concatenate([one, two, three], 0), high, contract)
    by_low = dot(jnp.concatenate([one, two], 0), low, contract)
    small_terms = by_high[rows : 2 * rows] + by_low[:rows]
    tiny_terms = by_high[2 * rows :] + by_low[rows:]
    return by_high[:rows] + (small_terms + tiny_terms)


def this_core():
    return lax.axis_index("dp") % 2


def in_vmem(x):
    return pltpu.with_memory_space_constraint(x, pltpu.VMEM)


whole = pl.BlockSpec(memory_space=pltpu.VMEM)
params = pltpu.CompilerParams(vmem_limit_bytes=16 * 1024 * 1024)


def in_hbm(x):
    return pltpu.with_memory_space_constraint(x, pltpu.HBM)


def left_kernel(grads, errors, q_t, terms, other, own, grads_here, errors_here, q_here, q_sem, grads_sem, errors_sem):
    layers, _, rows, _ = terms.shape
    core = this_core()
    pieces = [(l, b) for l in (1 - core, core) for b in range(rows // block_rows)]

    def fetch(n):
        l, b = pieces[n]
        at = pl.ds(b * block_rows, block_rows)
        return (
            pltpu.make_async_copy(grads.at[l, at], grads_here.at[l, at], grads_sem.at[n]),
            pltpu.make_async_copy(errors.at[l, at], errors_here.at[l, at], errors_sem.at[n]),
        )

    q_copy = pltpu.make_async_copy(q_t, q_here, q_sem)
    q_copy.start()
    for n in range(ahead):
        for copy in fetch(n):
            copy.start()
    q_copy.wait()
    for n, (l, b) in enumerate(pieces):
        for copy in fetch(n):
            copy.wait()
        if n + ahead < len(pieces):
            for copy in fetch(n + ahead):
                copy.start()
        at = pl.ds(b * block_rows, block_rows)
        merged = grads_here[l, at].astype(f32) + errors_here[l, at]
        merged_high, merged_low = halves(merged)
        terms[l, 0, at] = merged_high
        terms[l, 1, at] = merged_low
        term = split_dot(thirds(q_here[l]), merged_high, merged_low, ((1,), (1,)))
        part = other if n < len(pieces) // 2 else own
        for lane in range(block_rows // 128):
            part[b * (block_rows // 128) + lane] = term[:, lane * 128 : (lane + 1) * 128]


def left(grads, errors, q_t):
    layers, rows, cols = grads.shape
    rank = q_t.shape[1]
    pieces = layers * rows // block_rows
    return pl.pallas_call(
        left_kernel,
        in_specs=[pl.BlockSpec(memory_space=pltpu.HBM)] * 3,
        out_specs=[whole] * 3,
        out_shape=[
            pltpu.VMEM((layers, 2, rows, cols), bf16),
            pltpu.VMEM((rows // 128, rank, 128), f32),
            pltpu.VMEM((rows // 128, rank, 128), f32),
        ],
        scratch_shapes=[
            pltpu.VMEM(grads.shape, bf16),
            pltpu.VMEM(grads.shape, f32),
            pltpu.VMEM(q_t.shape, f32),
            pltpu.SemaphoreType.DMA,
            pltpu.SemaphoreType.DMA((pieces,)),
            pltpu.SemaphoreType.DMA((pieces,)),
        ],
        compiler_params=params,
        name="left",
    )(in_hbm(grads), in_hbm(errors), in_hbm(q_t))


def add(x, y, scale=1.0):
    def kernel(x, y, out):
        out[...] = (x[...] + y[...]) * scale

    return pl.pallas_call(
        kernel,
        in_specs=[whole] * 2,
        out_specs=whole,
        out_shape=pltpu.VMEM(x.shape, f32),
        compiler_params=params,
        name="add",
    )(in_vmem(x), in_vmem(y))


def right_kernel(terms, p_own, p_other, raw, gram, p_terms):
    layers = terms.shape[0]
    tiles, rank, _ = p_own.shape
    core = this_core()
    for l in range(layers):
        factor = jnp.concatenate([jnp.where(core == l, p_own[at], p_other[at]) for at in range(tiles)], 1)
        small = thirds(factor)
        term = split_dot(small, terms[l, 0], terms[l, 1], ((1,), (0,)))
        for at in range(raw.shape[1]):
            raw[l, at] = term[:, at * 128 : (at + 1) * 128]
        square = dot(factor, factor, ((1,), (1,)), highest)
        gram[l] = jnp.concatenate([square[at : at + 8] for at in range(0, rank, 8)], 1)
        stack = jnp.concatenate([small[0], small[1], small[0], jnp.zeros_like(small[0])], 0)
        p_terms[l] = stack.T


def right(terms, p_own, p_other):
    layers, _, rows, cols = terms.shape
    rank = p_own.shape[1]
    return pl.pallas_call(
        right_kernel,
        in_specs=[whole] * 3,
        out_specs=[whole] * 3,
        out_shape=[
            pltpu.VMEM((layers, cols // 128, rank, 128), f32),
            pltpu.VMEM((layers, 8, 128), f32),
            pltpu.VMEM((layers, rows, 4 * rank), bf16),
        ],
        compiler_params=params,
        name="right",
    )(in_vmem(terms), in_vmem(p_own), in_vmem(p_other))


def mix(raw, gram, copies):
    def kernel(raw, gram, out):
        total = jnp.sum(raw[...], axis=0)
        both = jnp.concatenate([total, gram[0], gram[1]], 0)
        out[...] = jnp.broadcast_to(both[None], out.shape)

    return pl.pallas_call(
        kernel,
        in_specs=[whole] * 2,
        out_specs=whole,
        out_shape=pltpu.VMEM((copies, raw.shape[1] + 16, 128), f32),
        compiler_params=params,
        name="mix",
    )(in_vmem(raw), in_vmem(gram))


def lower_inverses(packed, rank):
    groups = rank // 8
    row = lax.broadcasted_iota(jnp.int32, (8, 128), 0)
    lane = lax.broadcasted_iota(jnp.int32, (8, 128), 1)
    first = (lane // rank) % 2 == 0
    tiles = []
    for g in range(groups):
        squares = [tile[:, g * rank : (g + 1) * rank] for tile in packed]
        unit = (lane % rank == row + 8 * g).astype(f32)
        tiles.append(jnp.concatenate(squares + [unit[:, 2 * rank :]], 1))
    pivots = [jnp.ones((8, 128), f32)] * groups
    for start in range(0, rank, 16):
        columns = {}
        for k in range(start, start + 16):
            for g in range(start // 8, groups):
                columns[k, g] = jnp.where(first, tiles[g][:, k : k + 1], tiles[g][:, rank + k : rank + k + 1])
        for k in range(start, start + 16):
            at, s = divmod(k, 8)
            pivot = columns[k, at][s : s + 1]
            pivots[at] = jnp.where(row == s, pivot, pivots[at])
            over = 1.0 / pivot
            pivot_row = tiles[at][s : s + 1] * over
            entries = {j: columns[j, at][s : s + 1] * over for j in range(k + 1, start + 16)}
            for g in range(at, groups):
                column = columns[k, g]
                if g == at:
                    column = jnp.where(row > s, column, 0.0)
                tiles[g] = tiles[g] - column * pivot_row
                for j, entry in entries.items():
                    columns[j, g] = columns[j, g] - column * entry
    both = jnp.concatenate([tile / jnp.sqrt(pivot) for tile, pivot in zip(tiles, pivots)], 0)
    return [both[:, (2 + l) * rank : (3 + l) * rank] for l in range(2)]


def unmix(x, copies, rank, scale):
    def kernel(x, piece, inverse):
        total = jnp.sum(x[...], axis=0)
        piece[...] = jnp.broadcast_to(total[None, :8] * scale, piece.shape)
        inverse[0], inverse[1] = lower_inverses([total[8:16], total[16:24]], rank)

    return pl.pallas_call(
        kernel,
        in_specs=[whole],
        out_specs=[whole] * 2,
        out_shape=[pltpu.VMEM((copies, 8, 128), f32), pltpu.VMEM((2, rank, rank), f32)],
        compiler_params=params,
        name="unmix",
    )(in_vmem(x))


def last_kernel(
    terms, p_terms, inverse, raw, decompressed, new_errors, q_new,
    decompressed_here, errors_here, q_here, decompressed_sem, errors_sem, q_sem,
):
    layers, _, rows, _ = terms.shape
    copies = []

    def send(source, target, sem):
        copy = pltpu.make_async_copy(source, target, sem)
        copy.start()
        copies.append(copy)

    for l in range(layers):
        sums = jnp.concatenate([raw[l, at] for at in range(raw.shape[1])], 1)
        q = dot(inverse[l], sums, ((1,), (0,)), highest)
        q_here[l] = q
        send(q_here.at[l], q_new.at[l], q_sem.at[l])
        right_high, right_low = halves(dot(inverse[l], q, ((0,), (0,)), highest))
        stack = jnp.concatenate([right_high, right_high, right_low, jnp.zeros_like(right_high)], 0)
        for b in range(rows // block_rows):
            at = pl.ds(b * block_rows, block_rows)
            n = l * (rows // block_rows) + b
            approx = dot(p_terms[l, at], stack, ((1,), (0,)))
            decompressed_here[l, at] = approx.astype(bf16)
            errors_here[l, at] = (terms[l, 0, at].astype(f32) + terms[l, 1, at].astype(f32)) - approx
            send(decompressed_here.at[l, at], decompressed.at[l, at], decompressed_sem.at[n])
            send(errors_here.at[l, at], new_errors.at[l, at], errors_sem.at[n])
    for copy in copies:
        copy.wait()


def last(terms, p_terms, inverse, raw):
    layers, _, rows, cols = terms.shape
    shape = (layers, rows, cols)
    rank = inverse.shape[1]
    pieces = layers * rows // block_rows
    return pl.pallas_call(
        last_kernel,
        in_specs=[whole] * 4,
        out_specs=[pl.BlockSpec(memory_space=pltpu.HBM)] * 3,
        out_shape=[
            pltpu.HBM(shape, bf16),
            pltpu.HBM(shape, f32),
            pltpu.HBM((layers, rank, cols), f32),
        ],
        scratch_shapes=[
            pltpu.VMEM(shape, bf16),
            pltpu.VMEM(shape, f32),
            pltpu.VMEM((layers, rank, cols), f32),
            pltpu.SemaphoreType.DMA((pieces,)),
            pltpu.SemaphoreType.DMA((pieces,)),
            pltpu.SemaphoreType.DMA((layers,)),
        ],
        compiler_params=params,
        name="last",
    )(in_vmem(terms), in_vmem(p_terms), in_vmem(inverse), in_vmem(raw))


def exchange(x, axis):
    return lax.all_to_all(x, axis, 0, 0, tiled=True)


def swap(x, partner):
    replicas = lax.axis_size("dp")
    pairs = []
    for device in range(replicas):
        px, py, core = partner(device // 8, device // 2 % 4, device % 2)
        pairs.append((device, (px * 4 + py) * 2 + core))
    return lax.ppermute(x, "dp", pairs)


def sum_left(other, own, scale):
    total = add(own, swap(other, lambda x, y, core: (x, y, 1 - core)))
    for at, (first, second) in enumerate([((1, 0), (0, 1)), ((3, 0), (0, 3)), ((0, 1), (1, 0)), ((0, 3), (3, 0))]):

        def partner(x, y, core):
            dx, dy = (first, second)[core]
            return x ^ dx, y ^ dy, core

        total = add(total, swap(total, partner), scale if at == 3 else 1.0)
    return total, swap(total, lambda x, y, core: (x, y, 1 - core))


def on_device(grads, errors, q_prev):
    replicas, slabs, rank = lax.axis_size("dp"), lax.axis_size("tensor"), q_prev.shape[2]
    terms, other, own = left(grads[:, 0], errors[:, 0], jnp.swapaxes(q_prev, 1, 2))
    raw, gram, p_terms = right(terms, *sum_left(other, own, 1.0 / replicas))
    raw_shape = raw.shape
    raw = exchange(raw.reshape(replicas, -1, 128), "dp")
    both = exchange(mix(raw, gram, slabs), "tensor")
    raw, inverse = unmix(both, replicas, rank, 1.0 / replicas)
    raw = exchange(raw, "dp").reshape(raw_shape)
    decompressed, new_errors, q_new = last(terms, p_terms, inverse, raw)
    return decompressed, new_errors[:, None], jnp.swapaxes(q_new, 1, 2)


def solution(mesh):
    placed = (P(None, "dp", "tensor", None), P(None, "dp", "tensor", None), P())
    return jax.shard_map(
        on_device,
        mesh=mesh,
        in_specs=placed,
        out_specs=(P(None, "tensor", None), P(None, "dp", "tensor", None), P()),
        check_vma=False,
    )
```

```python
import jax
import jax.numpy as jnp
from jax import lax
from jax.experimental import pallas as pl
from jax.experimental.pallas import tpu as pltpu
from jax.sharding import PartitionSpec as P

highest = lax.Precision.HIGHEST
f32, bf16 = jnp.float32, jnp.bfloat16
block_rows = 512
ahead = 3


def halves(x):
    high = x.astype(bf16)
    return high, (x - high.astype(f32)).astype(bf16)


def thirds(x):
    high = x.astype(bf16)
    rest = x - high.astype(f32)
    return high, *halves(rest)


def dot(a, b, contract, precision=None):
    return lax.dot_general(a, b, (contract, ((), ())), precision=precision, preferred_element_type=f32)


def split_dot(small, high, low, contract):
    one, two, three = small
    rows = one.shape[0]
    by_high = dot(jnp.concatenate([one, two, three], 0), high, contract)
    by_low = dot(jnp.concatenate([one, two], 0), low, contract)
    small_terms = by_high[rows : 2 * rows] + by_low[:rows]
    tiny_terms = by_high[2 * rows :] + by_low[rows:]
    return by_high[:rows] + (small_terms + tiny_terms)


def this_core():
    return lax.axis_index("dp") % 2


def in_vmem(x):
    return pltpu.with_memory_space_constraint(x, pltpu.VMEM)


whole = pl.BlockSpec(memory_space=pltpu.VMEM)
params = pltpu.CompilerParams(vmem_limit_bytes=16 * 1024 * 1024)


def in_hbm(x):
    return pltpu.with_memory_space_constraint(x, pltpu.HBM)


def left_kernel(grads, errors, q_t, terms, other, own, grads_here, errors_here, q_here, q_sem, grads_sem, errors_sem):
    layers, _, rows, _ = terms.shape
    core = this_core()
    pieces = [(l, b) for l in (1 - core, core) for b in range(rows // block_rows)]

    def fetch(n):
        l, b = pieces[n]
        at = pl.ds(b * block_rows, block_rows)
        return (
            pltpu.make_async_copy(grads.at[l, at], grads_here.at[l, at], grads_sem.at[n]),
            pltpu.make_async_copy(errors.at[l, at], errors_here.at[l, at], errors_sem.at[n]),
        )

    q_copy = pltpu.make_async_copy(q_t, q_here, q_sem)
    q_copy.start()
    for n in range(ahead):
        for copy in fetch(n):
            copy.start()
    q_copy.wait()
    for n, (l, b) in enumerate(pieces):
        for copy in fetch(n):
            copy.wait()
        if n + ahead < len(pieces):
            for copy in fetch(n + ahead):
                copy.start()
        at = pl.ds(b * block_rows, block_rows)
        merged = grads_here[l, at].astype(f32) + errors_here[l, at]
        merged_high, merged_low = halves(merged)
        terms[l, 0, at] = merged_high
        terms[l, 1, at] = merged_low
        term = split_dot(thirds(q_here[l]), merged_high, merged_low, ((1,), (1,)))
        part = other if n < len(pieces) // 2 else own
        for lane in range(block_rows // 128):
            part[b * (block_rows // 128) + lane] = term[:, lane * 128 : (lane + 1) * 128]


def left(grads, errors, q_t):
    layers, rows, cols = grads.shape
    rank = q_t.shape[1]
    pieces = layers * rows // block_rows
    return pl.pallas_call(
        left_kernel,
        in_specs=[pl.BlockSpec(memory_space=pltpu.HBM)] * 3,
        out_specs=[whole] * 3,
        out_shape=[
            pltpu.VMEM((layers, 2, rows, cols), bf16),
            pltpu.VMEM((rows // 128, rank, 128), f32),
            pltpu.VMEM((rows // 128, rank, 128), f32),
        ],
        scratch_shapes=[
            pltpu.VMEM(grads.shape, bf16),
            pltpu.VMEM(grads.shape, f32),
            pltpu.VMEM(q_t.shape, f32),
            pltpu.SemaphoreType.DMA,
            pltpu.SemaphoreType.DMA((pieces,)),
            pltpu.SemaphoreType.DMA((pieces,)),
        ],
        compiler_params=params,
        name="left",
    )(in_hbm(grads), in_hbm(errors), in_hbm(q_t))


def add(terms, scale=1.0):
    def kernel(*refs):
        values = [ref[...] for ref in refs[:-1]]
        while len(values) > 1:
            values = [x + y for x, y in zip(values[::2], values[1::2])]
        refs[-1][...] = values[0] * scale

    return pl.pallas_call(
        kernel,
        in_specs=[whole] * len(terms),
        out_specs=whole,
        out_shape=pltpu.VMEM(terms[0].shape, f32),
        compiler_params=params,
        name="add",
    )(*[in_vmem(term) for term in terms])


def right_kernel(terms, p_own, p_other, raw, gram, p_terms):
    layers = terms.shape[0]
    tiles, rank, _ = p_own.shape
    core = this_core()
    for l in range(layers):
        factor = jnp.concatenate([jnp.where(core == l, p_own[at], p_other[at]) for at in range(tiles)], 1)
        small = thirds(factor)
        term = split_dot(small, terms[l, 0], terms[l, 1], ((1,), (0,)))
        for at in range(raw.shape[1]):
            raw[l, at] = term[:, at * 128 : (at + 1) * 128]
        square = dot(factor, factor, ((1,), (1,)), highest)
        gram[l] = jnp.concatenate([square[at : at + 8] for at in range(0, rank, 8)], 1)
        stack = jnp.concatenate([small[0], small[1], small[0], jnp.zeros_like(small[0])], 0)
        p_terms[l] = stack.T


def right(terms, p_own, p_other):
    layers, _, rows, cols = terms.shape
    rank = p_own.shape[1]
    return pl.pallas_call(
        right_kernel,
        in_specs=[whole] * 3,
        out_specs=[whole] * 3,
        out_shape=[
            pltpu.VMEM((layers, cols // 128, rank, 128), f32),
            pltpu.VMEM((layers, 8, 128), f32),
            pltpu.VMEM((layers, rows, 4 * rank), bf16),
        ],
        compiler_params=params,
        name="right",
    )(in_vmem(terms), in_vmem(p_own), in_vmem(p_other))


def mix(raw, gram, copies):
    def kernel(raw, gram, out):
        total = jnp.sum(raw[...], axis=0)
        both = jnp.concatenate([total, gram[0], gram[1]], 0)
        out[...] = jnp.broadcast_to(both[None], out.shape)

    return pl.pallas_call(
        kernel,
        in_specs=[whole] * 2,
        out_specs=whole,
        out_shape=pltpu.VMEM((copies, raw.shape[1] + 16, 128), f32),
        compiler_params=params,
        name="mix",
    )(in_vmem(raw), in_vmem(gram))


def lower_inverses(packed, rank):
    groups = rank // 8
    row = lax.broadcasted_iota(jnp.int32, (8, 128), 0)
    lane = lax.broadcasted_iota(jnp.int32, (8, 128), 1)
    first = (lane // rank) % 2 == 0
    tiles = []
    for g in range(groups):
        squares = [tile[:, g * rank : (g + 1) * rank] for tile in packed]
        unit = (lane % rank == row + 8 * g).astype(f32)
        tiles.append(jnp.concatenate(squares + [unit[:, 2 * rank :]], 1))
    pivots = [jnp.ones((8, 128), f32)] * groups
    for start in range(0, rank, 16):
        columns = {}
        for k in range(start, start + 16):
            for g in range(start // 8, groups):
                columns[k, g] = jnp.where(first, tiles[g][:, k : k + 1], tiles[g][:, rank + k : rank + k + 1])
        for k in range(start, start + 16):
            at, s = divmod(k, 8)
            pivot = columns[k, at][s : s + 1]
            pivots[at] = jnp.where(row == s, pivot, pivots[at])
            over = 1.0 / pivot
            pivot_row = tiles[at][s : s + 1] * over
            entries = {j: columns[j, at][s : s + 1] * over for j in range(k + 1, start + 16)}
            for g in range(at, groups):
                column = columns[k, g]
                if g == at:
                    column = jnp.where(row > s, column, 0.0)
                tiles[g] = tiles[g] - column * pivot_row
                for j, entry in entries.items():
                    columns[j, g] = columns[j, g] - column * entry
    both = jnp.concatenate([tile / jnp.sqrt(pivot) for tile, pivot in zip(tiles, pivots)], 0)
    return [both[:, (2 + l) * rank : (3 + l) * rank] for l in range(2)]


def unmix(x, copies, rank, scale):
    def kernel(x, piece, inverse):
        total = jnp.sum(x[...], axis=0)
        piece[...] = jnp.broadcast_to(total[None, :8] * scale, piece.shape)
        inverse[0], inverse[1] = lower_inverses([total[8:16], total[16:24]], rank)

    return pl.pallas_call(
        kernel,
        in_specs=[whole],
        out_specs=[whole] * 2,
        out_shape=[pltpu.VMEM((copies, 8, 128), f32), pltpu.VMEM((2, rank, rank), f32)],
        compiler_params=params,
        name="unmix",
    )(in_vmem(x))


def last_kernel(
    terms, p_terms, inverse, raw, decompressed, new_errors, q_new,
    decompressed_here, errors_here, q_here, decompressed_sem, errors_sem, q_sem,
):
    layers, _, rows, _ = terms.shape
    copies = []

    def send(source, target, sem):
        copy = pltpu.make_async_copy(source, target, sem)
        copy.start()
        copies.append(copy)

    for l in range(layers):
        sums = jnp.concatenate([raw[l, at] for at in range(raw.shape[1])], 1)
        q = dot(inverse[l], sums, ((1,), (0,)), highest)
        q_here[l] = q
        send(q_here.at[l], q_new.at[l], q_sem.at[l])
        right_high, right_low = halves(dot(inverse[l], q, ((0,), (0,)), highest))
        stack = jnp.concatenate([right_high, right_high, right_low, jnp.zeros_like(right_high)], 0)
        for b in range(rows // block_rows):
            at = pl.ds(b * block_rows, block_rows)
            n = l * (rows // block_rows) + b
            approx = dot(p_terms[l, at], stack, ((1,), (0,)))
            decompressed_here[l, at] = approx.astype(bf16)
            errors_here[l, at] = (terms[l, 0, at].astype(f32) + terms[l, 1, at].astype(f32)) - approx
            send(decompressed_here.at[l, at], decompressed.at[l, at], decompressed_sem.at[n])
            send(errors_here.at[l, at], new_errors.at[l, at], errors_sem.at[n])
    for copy in copies:
        copy.wait()


def last(terms, p_terms, inverse, raw):
    layers, _, rows, cols = terms.shape
    shape = (layers, rows, cols)
    rank = inverse.shape[1]
    pieces = layers * rows // block_rows
    return pl.pallas_call(
        last_kernel,
        in_specs=[whole] * 4,
        out_specs=[pl.BlockSpec(memory_space=pltpu.HBM)] * 3,
        out_shape=[
            pltpu.HBM(shape, bf16),
            pltpu.HBM(shape, f32),
            pltpu.HBM((layers, rank, cols), f32),
        ],
        scratch_shapes=[
            pltpu.VMEM(shape, bf16),
            pltpu.VMEM(shape, f32),
            pltpu.VMEM((layers, rank, cols), f32),
            pltpu.SemaphoreType.DMA((pieces,)),
            pltpu.SemaphoreType.DMA((pieces,)),
            pltpu.SemaphoreType.DMA((layers,)),
        ],
        compiler_params=params,
        name="last",
    )(in_vmem(terms), in_vmem(p_terms), in_vmem(inverse), in_vmem(raw))


def exchange(x, axis):
    return lax.all_to_all(x, axis, 0, 0, tiled=True)


def swap(x, partner):
    replicas = lax.axis_size("dp")
    pairs = []
    for device in range(replicas):
        px, py, core = partner(device // 8, device // 2 % 4, device % 2)
        pairs.append((device, (px * 4 + py) * 2 + core))
    return lax.ppermute(x, "dp", pairs)


def sum_left(other, own, scale):
    total = add([own, swap(other, lambda x, y, core: (x, y, 1 - core))])
    for axis, factor in (0, 1.0), (1, scale):
        near, wrap, far = (
            swap(total, lambda x, y, core, to=to: (x ^ to, y, core) if axis == 0 else (x, y ^ to, core))
            for to in (1, 3, 2)
        )
        total = add([total, near, wrap, far], factor)
    return total, swap(total, lambda x, y, core: (x, y, 1 - core))


def on_device(grads, errors, q_prev):
    replicas, slabs, rank = lax.axis_size("dp"), lax.axis_size("tensor"), q_prev.shape[2]
    terms, other, own = left(grads[:, 0], errors[:, 0], jnp.swapaxes(q_prev, 1, 2))
    raw, gram, p_terms = right(terms, *sum_left(other, own, 1.0 / replicas))
    raw_shape = raw.shape
    raw = exchange(raw.reshape(replicas, -1, 128), "dp")
    both = exchange(mix(raw, gram, slabs), "tensor")
    raw, inverse = unmix(both, replicas, rank, 1.0 / replicas)
    raw = exchange(raw, "dp").reshape(raw_shape)
    decompressed, new_errors, q_new = last(terms, p_terms, inverse, raw)
    return decompressed, new_errors[:, None], jnp.swapaxes(q_new, 1, 2)


def solution(mesh):
    placed = (P(None, "dp", "tensor", None), P(None, "dp", "tensor", None), P())
    return jax.shard_map(
        on_device,
        mesh=mesh,
        in_specs=placed,
        out_specs=(P(None, "tensor", None), P(None, "dp", "tensor", None), P()),
        check_vma=False,
    )
```

```python
import jax
import jax.numpy as jnp
from jax import lax
from jax.experimental import pallas as pl
from jax.experimental.pallas import tpu as pltpu
from jax.sharding import PartitionSpec as P

highest = lax.Precision.HIGHEST
f32, bf16 = jnp.float32, jnp.bfloat16
block_rows = 512
ahead = 3
last_pieces = {True: [(0, 256), (256, 512), (512, 1024)], False: [(0, 512), (512, 1024)]}


def halves(x):
    high = x.astype(bf16)
    return high, (x - high.astype(f32)).astype(bf16)


def thirds(x):
    high = x.astype(bf16)
    rest = x - high.astype(f32)
    return high, *halves(rest)


def dot(a, b, contract, precision=None):
    return lax.dot_general(a, b, (contract, ((), ())), precision=precision, preferred_element_type=f32)


def split_dot(small, high, low, contract):
    one, two, three = small
    rows = one.shape[0]
    by_high = dot(jnp.concatenate([one, two, three], 0), high, contract)
    by_low = dot(jnp.concatenate([one, two], 0), low, contract)
    small_terms = by_high[rows : 2 * rows] + by_low[:rows]
    tiny_terms = by_high[2 * rows :] + by_low[rows:]
    return by_high[:rows] + (small_terms + tiny_terms)


def this_core():
    return lax.axis_index("dp") % 2


def in_vmem(x):
    return pltpu.with_memory_space_constraint(x, pltpu.VMEM)


whole = pl.BlockSpec(memory_space=pltpu.VMEM)
params = pltpu.CompilerParams(vmem_limit_bytes=16 * 1024 * 1024)


def in_hbm(x):
    return pltpu.with_memory_space_constraint(x, pltpu.HBM)


def left_kernel(grads, errors, q_t, terms, merged_other, other, own, grads_here, errors_here, q_here, q_sem, grads_sem, errors_sem):
    layers, _, rows, _ = terms.shape
    core = this_core()
    pieces = [(l, b) for l in (1 - core, core) for b in range(rows // block_rows)]

    def fetch(n):
        l, b = pieces[n]
        at = pl.ds(b * block_rows, block_rows)
        return (
            pltpu.make_async_copy(grads.at[l, at], grads_here.at[l, at], grads_sem.at[n]),
            pltpu.make_async_copy(errors.at[l, at], errors_here.at[l, at], errors_sem.at[n]),
        )

    q_copy = pltpu.make_async_copy(q_t, q_here, q_sem)
    q_copy.start()
    for n in range(ahead):
        for copy in fetch(n):
            copy.start()
    q_copy.wait()
    for n, (l, b) in enumerate(pieces):
        for copy in fetch(n):
            copy.wait()
        if n + ahead < len(pieces):
            for copy in fetch(n + ahead):
                copy.start()
        at = pl.ds(b * block_rows, block_rows)
        merged = grads_here[l, at].astype(f32) + errors_here[l, at]
        if n < len(pieces) // 2:
            merged_other[at] = merged
        merged_high, merged_low = halves(merged)
        terms[l, 0, at] = merged_high
        terms[l, 1, at] = merged_low
        term = split_dot(thirds(q_here[l]), merged_high, merged_low, ((1,), (1,)))
        part = other if n < len(pieces) // 2 else own
        for lane in range(block_rows // 128):
            part[b * (block_rows // 128) + lane] = term[:, lane * 128 : (lane + 1) * 128]


def left(grads, errors, q_t):
    layers, rows, cols = grads.shape
    rank = q_t.shape[1]
    pieces = layers * rows // block_rows
    return pl.pallas_call(
        left_kernel,
        in_specs=[pl.BlockSpec(memory_space=pltpu.HBM)] * 3,
        out_specs=[whole] * 4,
        out_shape=[
            pltpu.VMEM((layers, 2, rows, cols), bf16),
            pltpu.VMEM((rows, cols), f32),
            pltpu.VMEM((rows // 128, rank, 128), f32),
            pltpu.VMEM((rows // 128, rank, 128), f32),
        ],
        scratch_shapes=[
            pltpu.VMEM(grads.shape, bf16),
            pltpu.VMEM(grads.shape, f32),
            pltpu.VMEM(q_t.shape, f32),
            pltpu.SemaphoreType.DMA,
            pltpu.SemaphoreType.DMA((pieces,)),
            pltpu.SemaphoreType.DMA((pieces,)),
        ],
        compiler_params=params,
        name="left",
    )(in_hbm(grads), in_hbm(errors), in_hbm(q_t))


def add(terms, scale=1.0):
    def kernel(*refs):
        values = [ref[...] for ref in refs[:-1]]
        while len(values) > 1:
            values = [x + y for x, y in zip(values[::2], values[1::2])]
        refs[-1][...] = values[0] * scale

    return pl.pallas_call(
        kernel,
        in_specs=[whole] * len(terms),
        out_specs=whole,
        out_shape=pltpu.VMEM(terms[0].shape, f32),
        compiler_params=params,
        name="add",
    )(*[in_vmem(term) for term in terms])


def pair(terms, merged):
    _, _, rows, cols = terms.shape

    def kernel(terms, merged, out):
        core = this_core()
        both = (terms[core, 0].astype(f32) + terms[core, 1].astype(f32)) + merged[...]
        out[0], out[1] = halves(both)

    return pl.pallas_call(
        kernel,
        in_specs=[whole] * 2,
        out_specs=whole,
        out_shape=pltpu.VMEM((2, rows, cols), bf16),
        compiler_params=params,
        cost_estimate=pl.CostEstimate(flops=4_000_000, bytes_accessed=6 * 1024 * 1024, transcendentals=0),
        name="pair",
    )(in_vmem(terms), in_vmem(merged))


def stack_terms(one, two):
    return jnp.concatenate([one, two, one, jnp.zeros_like(one)], 0).T


def packed_gram(factor):
    rank = factor.shape[0]
    square = dot(factor, factor, ((1,), (1,)), highest)
    return jnp.concatenate([square[at : at + 8] for at in range(0, rank, 8)], 1)


def right_kernel(pair_terms, p_t, raw, gram, p_terms):
    tiles, rank, _ = p_t.shape
    factor = jnp.concatenate([p_t[at] for at in range(tiles)], 1)
    small = thirds(factor)
    term = split_dot(small, pair_terms[0], pair_terms[1], ((1,), (0,)))
    for at in range(raw.shape[0]):
        raw[at] = term[:, at * 128 : (at + 1) * 128]
    gram[...] = packed_gram(factor)
    p_terms[...] = stack_terms(*small[:2])


def right(pair_terms, p_t):
    _, rows, cols = pair_terms.shape
    rank = p_t.shape[1]
    return pl.pallas_call(
        right_kernel,
        in_specs=[whole] * 2,
        out_specs=[whole] * 3,
        out_shape=[
            pltpu.VMEM((cols // 128, rank, 128), f32),
            pltpu.VMEM((8, 128), f32),
            pltpu.VMEM((rows, 4 * rank), bf16),
        ],
        compiler_params=params,
        name="right",
    )(in_vmem(pair_terms), in_vmem(p_t))


def mix(raw, gram, p_other, copies):
    def kernel(raw, gram, p_other, out):
        factor = jnp.concatenate([p_other[at] for at in range(p_other.shape[0])], 1)
        both = jnp.concatenate([jnp.sum(raw[...], axis=0), gram[...], packed_gram(factor)], 0)
        out[...] = jnp.broadcast_to(both[None], out.shape)

    return pl.pallas_call(
        kernel,
        in_specs=[whole] * 3,
        out_specs=whole,
        out_shape=pltpu.VMEM((copies, 24, 128), f32),
        compiler_params=params,
        name="mix",
    )(in_vmem(raw), in_vmem(gram), in_vmem(p_other))


def lower_inverses(packed, rank):
    groups = rank // 8
    row = lax.broadcasted_iota(jnp.int32, (8, 128), 0)
    lane = lax.broadcasted_iota(jnp.int32, (8, 128), 1)
    first = (lane // rank) % 2 == 0
    tiles = []
    for g in range(groups):
        squares = [tile[:, g * rank : (g + 1) * rank] for tile in packed]
        unit = (lane % rank == row + 8 * g).astype(f32)
        tiles.append(jnp.concatenate(squares + [unit[:, 2 * rank :]], 1))
    pivots = [jnp.ones((8, 128), f32)] * groups
    for start in range(0, rank, 16):
        columns = {}
        for k in range(start, start + 16):
            for g in range(start // 8, groups):
                columns[k, g] = jnp.where(first, tiles[g][:, k : k + 1], tiles[g][:, rank + k : rank + k + 1])
        for k in range(start, start + 16):
            at, s = divmod(k, 8)
            pivot = columns[k, at][s : s + 1]
            pivots[at] = jnp.where(row == s, pivot, pivots[at])
            over = 1.0 / pivot
            pivot_row = tiles[at][s : s + 1] * over
            entries = {j: columns[j, at][s : s + 1] * over for j in range(k + 1, start + 16)}
            for g in range(at, groups):
                column = columns[k, g]
                if g == at:
                    column = jnp.where(row > s, column, 0.0)
                tiles[g] = tiles[g] - column * pivot_row
                for j, entry in entries.items():
                    columns[j, g] = columns[j, g] - column * entry
    both = jnp.concatenate([tile / jnp.sqrt(pivot) for tile, pivot in zip(tiles, pivots)], 0)
    return [both[:, (2 + l) * rank : (3 + l) * rank] for l in range(2)]


def unmix(x, copies, rank, scale):
    def kernel(x, piece, inverse):
        total = jnp.sum(x[...], axis=0)
        piece[...] = jnp.broadcast_to(total[None, :8] * scale, piece.shape)
        inverse[0], inverse[1] = lower_inverses([total[8:16], total[16:24]], rank)

    return pl.pallas_call(
        kernel,
        in_specs=[whole],
        out_specs=[whole] * 2,
        out_shape=[pltpu.VMEM((copies, 8, 128), f32), pltpu.VMEM((2, rank, rank), f32)],
        compiler_params=params,
        name="unmix",
    )(in_vmem(x))


def last_kernel(
    terms, p_terms, p_other, inverse, raw, decompressed, new_errors, q_new,
    decompressed_here, errors_here, q_here, decompressed_sem, errors_sem, q_sem,
):
    _, _, rows, cols = terms.shape
    rank = inverse.shape[1]
    core = this_core()
    copies = []

    def send(source, target, sem):
        copy = pltpu.make_async_copy(source, target, sem)
        copy.start()
        copies.append(copy)

    for own in (True, False):
        l = core if own else 1 - core
        lower = inverse[0 if own else 1]
        lanes = [[raw[2 * (j * rank // 8 + i) + l] for i in range(rank // 8)] for j in range(cols // 128)]
        sums = jnp.concatenate([jnp.concatenate(tiles, 0) for tiles in lanes], 1)
        q = dot(lower, sums, ((1,), (0,)), highest)
        q_here[l] = q
        send(q_here.at[l], q_new.at[l], q_sem.at[0 if own else 1])
        right_high, right_low = halves(dot(lower, q, ((0,), (0,)), highest))
        stack = jnp.concatenate([right_high, right_high, right_low, jnp.zeros_like(right_high)], 0)
        for n, (start, end) in enumerate(last_pieces[own]):
            at = pl.ds(start, end - start)
            if own:
                left_rows = p_terms[at]
            else:
                tiles = [p_other[tile] for tile in range(start // 128, end // 128)]
                left_rows = stack_terms(*halves(jnp.concatenate(tiles, 1)))
            approx = dot(left_rows, stack, ((1,), (0,)))
            decompressed_here[l, at] = approx.astype(bf16)
            errors_here[l, at] = (terms[l, 0, at].astype(f32) + terms[l, 1, at].astype(f32)) - approx
            sem = n if own else len(last_pieces[True]) + n
            send(decompressed_here.at[l, at], decompressed.at[l, at], decompressed_sem.at[sem])
            send(errors_here.at[l, at], new_errors.at[l, at], errors_sem.at[sem])
    for copy in copies:
        copy.wait()


def last(terms, p_terms, p_other, inverse, raw):
    layers, _, rows, cols = terms.shape
    shape = (layers, rows, cols)
    rank = inverse.shape[1]
    pieces = len(last_pieces[True]) + len(last_pieces[False])
    return pl.pallas_call(
        last_kernel,
        in_specs=[whole] * 5,
        out_specs=[pl.BlockSpec(memory_space=pltpu.HBM)] * 3,
        out_shape=[
            pltpu.HBM(shape, bf16),
            pltpu.HBM(shape, f32),
            pltpu.HBM((layers, rank, cols), f32),
        ],
        scratch_shapes=[
            pltpu.VMEM(shape, bf16),
            pltpu.VMEM(shape, f32),
            pltpu.VMEM((layers, rank, cols), f32),
            pltpu.SemaphoreType.DMA((pieces,)),
            pltpu.SemaphoreType.DMA((pieces,)),
            pltpu.SemaphoreType.DMA((layers,)),
        ],
        compiler_params=params,
        name="last",
    )(*[in_vmem(x) for x in (terms, p_terms, p_other, inverse, raw)])


def exchange(x, axis, groups=None):
    return lax.all_to_all(x, axis, 0, 0, axis_index_groups=groups, tiled=True)


def swap(x, partner):
    replicas = lax.axis_size("dp")
    pairs = []
    for device in range(replicas):
        px, py, core = partner(device // 8, device // 2 % 4, device % 2)
        pairs.append((device, (px * 4 + py) * 2 + core))
    return lax.ppermute(x, "dp", pairs)


def swap_cores(x):
    return swap(x, lambda x, y, core: (x, y, 1 - core))


def sum_axis(total, axis, scale):
    near, wrap, far = (
        swap(total, lambda x, y, core, to=to: (x ^ to, y, core) if axis == 0 else (x, y ^ to, core))
        for to in (1, 3, 2)
    )
    return add([total, near, wrap, far], scale)


def on_device(grads, errors, q_prev):
    replicas, slabs, rank = lax.axis_size("dp"), lax.axis_size("tensor"), q_prev.shape[2]
    terms, merged, other, own = left(grads[:, 0], errors[:, 0], jnp.swapaxes(q_prev, 1, 2))
    total, merged = lax.optimization_barrier((add([own, swap_cores(other)]), merged))
    pair_terms = pair(terms, swap_cores(merged))
    p_t = sum_axis(sum_axis(total, 0, 1.0), 1, 1.0 / replicas)
    raw, gram, p_terms = right(pair_terms, p_t)
    raw, p_other = lax.optimization_barrier((raw, swap_cores(p_t)))
    chips = [[2 * chip + core for chip in range(replicas // 2)] for core in range(2)]
    raw = exchange(raw.reshape(replicas // 2, 8, 128), "dp", chips)
    both = exchange(mix(raw, gram, p_other, slabs), "tensor")
    raw, inverse = unmix(both, replicas, rank, 1.0 / replicas)
    decompressed, new_errors, q_new = last(terms, p_terms, p_other, inverse, exchange(raw, "dp"))
    return decompressed, new_errors[:, None], jnp.swapaxes(q_new, 1, 2)


def solution(mesh):
    placed = (P(None, "dp", "tensor", None), P(None, "dp", "tensor", None), P())
    return jax.shard_map(
        on_device,
        mesh=mesh,
        in_specs=placed,
        out_specs=(P(None, "tensor", None), P(None, "dp", "tensor", None), P()),
        check_vma=False,
    )
```

```python
import jax
import jax.numpy as jnp
from jax import lax
from jax.experimental import pallas as pl
from jax.experimental.pallas import tpu as pltpu
from jax.sharding import PartitionSpec as P

highest = lax.Precision.HIGHEST
f32, bf16 = jnp.float32, jnp.bfloat16
block_rows = 512
ahead = 3
last_pieces = {True: [(0, 256), (256, 512), (512, 1024)], False: [(0, 512), (512, 1024)]}


def halves(x):
    high = x.astype(bf16)
    return high, (x - high.astype(f32)).astype(bf16)


def thirds(x):
    high = x.astype(bf16)
    rest = x - high.astype(f32)
    return high, *halves(rest)


def dot(a, b, contract, precision=None):
    return lax.dot_general(a, b, (contract, ((), ())), precision=precision, preferred_element_type=f32)


def split_dot(small, high, low, contract):
    one, two, three = small
    rows = one.shape[0]
    by_high = dot(jnp.concatenate([one, two, three], 0), high, contract)
    by_low = dot(jnp.concatenate([one, two], 0), low, contract)
    small_terms = by_high[rows : 2 * rows] + by_low[:rows]
    tiny_terms = by_high[2 * rows :] + by_low[rows:]
    return by_high[:rows] + (small_terms + tiny_terms)


def this_core():
    return lax.axis_index("dp") % 2


def in_vmem(x):
    return pltpu.with_memory_space_constraint(x, pltpu.VMEM)


whole = pl.BlockSpec(memory_space=pltpu.VMEM)
params = pltpu.CompilerParams(vmem_limit_bytes=16 * 1024 * 1024)


def in_hbm(x):
    return pltpu.with_memory_space_constraint(x, pltpu.HBM)


def left_kernel(grads, errors, q_t, terms, merged_other, other, own, grads_here, errors_here, q_here, q_sem, grads_sem, errors_sem):
    layers, _, rows, _ = terms.shape
    core = this_core()
    pieces = [(l, b) for l in (1 - core, core) for b in range(rows // block_rows)]

    def fetch(n):
        l, b = pieces[n]
        at = pl.ds(b * block_rows, block_rows)
        return (
            pltpu.make_async_copy(grads.at[l, at], grads_here.at[l, at], grads_sem.at[n]),
            pltpu.make_async_copy(errors.at[l, at], errors_here.at[l, at], errors_sem.at[n]),
        )

    q_copy = pltpu.make_async_copy(q_t, q_here, q_sem)
    q_copy.start()
    for n in range(ahead):
        for copy in fetch(n):
            copy.start()
    q_copy.wait()
    for n, (l, b) in enumerate(pieces):
        for copy in fetch(n):
            copy.wait()
        if n + ahead < len(pieces):
            for copy in fetch(n + ahead):
                copy.start()
        at = pl.ds(b * block_rows, block_rows)
        merged = grads_here[l, at].astype(f32) + errors_here[l, at]
        if n < len(pieces) // 2:
            merged_other[at] = merged
        merged_high, merged_low = halves(merged)
        terms[l, 0, at] = merged_high
        terms[l, 1, at] = merged_low
        term = split_dot(thirds(q_here[l]), merged_high, merged_low, ((1,), (1,)))
        part = other if n < len(pieces) // 2 else own
        for lane in range(block_rows // 128):
            part[b * (block_rows // 128) + lane] = term[:, lane * 128 : (lane + 1) * 128]


def left(grads, errors, q_t):
    layers, rows, cols = grads.shape
    rank = q_t.shape[1]
    pieces = layers * rows // block_rows
    return pl.pallas_call(
        left_kernel,
        in_specs=[pl.BlockSpec(memory_space=pltpu.HBM)] * 3,
        out_specs=[whole] * 4,
        out_shape=[
            pltpu.VMEM((layers, 2, rows, cols), bf16),
            pltpu.VMEM((rows, cols), f32),
            pltpu.VMEM((rows // 128, rank, 128), f32),
            pltpu.VMEM((rows // 128, rank, 128), f32),
        ],
        scratch_shapes=[
            pltpu.VMEM(grads.shape, bf16),
            pltpu.VMEM(grads.shape, f32),
            pltpu.VMEM(q_t.shape, f32),
            pltpu.SemaphoreType.DMA,
            pltpu.SemaphoreType.DMA((pieces,)),
            pltpu.SemaphoreType.DMA((pieces,)),
        ],
        compiler_params=params,
        name="left",
    )(in_hbm(grads), in_hbm(errors), in_hbm(q_t))


def add(terms, scale=1.0):
    def kernel(*refs):
        values = [ref[...] for ref in refs[:-1]]
        while len(values) > 1:
            values = [x + y for x, y in zip(values[::2], values[1::2])]
        refs[-1][...] = values[0] * scale

    return pl.pallas_call(
        kernel,
        in_specs=[whole] * len(terms),
        out_specs=whole,
        out_shape=pltpu.VMEM(terms[0].shape, f32),
        compiler_params=params,
        name="add",
    )(*[in_vmem(term) for term in terms])


def pair(terms, merged):
    _, _, rows, cols = terms.shape

    def kernel(terms, merged, out):
        core = this_core()
        both = (terms[core, 0].astype(f32) + terms[core, 1].astype(f32)) + merged[...]
        out[0], out[1] = halves(both)

    return pl.pallas_call(
        kernel,
        in_specs=[whole] * 2,
        out_specs=whole,
        out_shape=pltpu.VMEM((2, rows, cols), bf16),
        compiler_params=params,
        cost_estimate=pl.CostEstimate(flops=4_000_000, bytes_accessed=6 * 1024 * 1024, transcendentals=0),
        name="pair",
    )(in_vmem(terms), in_vmem(merged))


def stack_terms(one, two):
    return jnp.concatenate([one, two, one, jnp.zeros_like(one)], 0).T


def packed_gram(factor):
    rank = factor.shape[0]
    square = dot(factor, factor, ((1,), (1,)), highest)
    return jnp.concatenate([square[at : at + 8] for at in range(0, rank, 8)], 1)


def right_kernel(pair_terms, p_t, raw, gram, p_terms):
    tiles, rank, _ = p_t.shape
    factor = jnp.concatenate([p_t[at] for at in range(tiles)], 1)
    small = thirds(factor)
    term = split_dot(small, pair_terms[0], pair_terms[1], ((1,), (0,)))
    for at in range(raw.shape[0]):
        raw[at] = term[:, at * 128 : (at + 1) * 128]
    gram[...] = packed_gram(factor)
    p_terms[...] = stack_terms(*small[:2])


def right(pair_terms, p_t):
    _, rows, cols = pair_terms.shape
    rank = p_t.shape[1]
    return pl.pallas_call(
        right_kernel,
        in_specs=[whole] * 2,
        out_specs=[whole] * 3,
        out_shape=[
            pltpu.VMEM((cols // 128, rank, 128), f32),
            pltpu.VMEM((8, 128), f32),
            pltpu.VMEM((rows, 4 * rank), bf16),
        ],
        compiler_params=params,
        name="right",
    )(in_vmem(pair_terms), in_vmem(p_t))


def mix(raw, gram, p_other, copies):
    def kernel(raw, gram, p_other, out):
        factor = jnp.concatenate([p_other[at] for at in range(p_other.shape[0])], 1)
        both = jnp.concatenate([jnp.sum(raw[...], axis=0), gram[...], packed_gram(factor)], 0)
        out[...] = jnp.broadcast_to(both[None], out.shape)

    return pl.pallas_call(
        kernel,
        in_specs=[whole] * 3,
        out_specs=whole,
        out_shape=pltpu.VMEM((copies, 24, 128), f32),
        compiler_params=params,
        name="mix",
    )(in_vmem(raw), in_vmem(gram), in_vmem(p_other))


def lower_inverses(packed, rank):
    groups = rank // 8
    row = lax.broadcasted_iota(jnp.int32, (8, 128), 0)
    lane = lax.broadcasted_iota(jnp.int32, (8, 128), 1)
    first = (lane // rank) % 2 == 0
    tiles = []
    for g in range(groups):
        squares = [tile[:, g * rank : (g + 1) * rank] for tile in packed]
        unit = (lane % rank == row + 8 * g).astype(f32)
        tiles.append(jnp.concatenate(squares + [unit[:, 2 * rank :]], 1))
    pivots = [jnp.ones((8, 128), f32)] * groups
    for start in range(0, rank, 16):
        columns = {}
        for k in range(start, start + 16):
            for g in range(start // 8, groups):
                columns[k, g] = jnp.where(first, tiles[g][:, k : k + 1], tiles[g][:, rank + k : rank + k + 1])
        for k in range(start, start + 16):
            at, s = divmod(k, 8)
            pivot = columns[k, at][s : s + 1]
            pivots[at] = jnp.where(row == s, pivot, pivots[at])
            over = 1.0 / pivot
            pivot_row = tiles[at][s : s + 1] * over
            entries = {j: columns[j, at][s : s + 1] * over for j in range(k + 1, start + 16)}
            for g in range(at, groups):
                column = columns[k, g]
                if g == at:
                    column = jnp.where(row > s, column, 0.0)
                tiles[g] = tiles[g] - column * pivot_row
                for j, entry in entries.items():
                    columns[j, g] = columns[j, g] - column * entry
    both = jnp.concatenate([tile / jnp.sqrt(pivot) for tile, pivot in zip(tiles, pivots)], 0)
    return [both[:, (2 + l) * rank : (3 + l) * rank] for l in range(2)]


def unmix(x, copies, rank, scale):
    def kernel(x, piece, inverse):
        total = jnp.sum(x[...], axis=0)
        piece[...] = jnp.broadcast_to(total[None, :8] * scale, piece.shape)
        inverse[0], inverse[1] = lower_inverses([total[8:16], total[16:24]], rank)

    return pl.pallas_call(
        kernel,
        in_specs=[whole],
        out_specs=[whole] * 2,
        out_shape=[pltpu.VMEM((copies, 8, 128), f32), pltpu.VMEM((2, rank, rank), f32)],
        compiler_params=params,
        name="unmix",
    )(in_vmem(x))


def last_kernel(
    terms, p_terms, p_other, inverse, raw, decompressed, new_errors, q_new,
    decompressed_here, errors_here, q_here, decompressed_sem, errors_sem, q_sem,
):
    _, _, rows, cols = terms.shape
    rank = inverse.shape[1]
    core = this_core()
    copies = []

    def send(source, target, sem):
        copy = pltpu.make_async_copy(source, target, sem)
        copy.start()
        copies.append(copy)

    for own in (True, False):
        l = core if own else 1 - core
        lower = inverse[0 if own else 1]
        lanes = [[raw[2 * (j * rank // 8 + i) + l] for i in range(rank // 8)] for j in range(cols // 128)]
        sums = jnp.concatenate([jnp.concatenate(tiles, 0) for tiles in lanes], 1)
        q = dot(lower, sums, ((1,), (0,)), highest)
        q_here[l] = q
        send(q_here.at[l], q_new.at[l], q_sem.at[0 if own else 1])
        right_high, right_low = halves(dot(lower, q, ((0,), (0,)), highest))
        stack = jnp.concatenate([right_high, right_high, right_low, jnp.zeros_like(right_high)], 0)
        for n, (start, end) in enumerate(last_pieces[own]):
            at = pl.ds(start, end - start)
            if own:
                left_rows = p_terms[at]
            else:
                tiles = [p_other[tile] for tile in range(start // 128, end // 128)]
                left_rows = stack_terms(*halves(jnp.concatenate(tiles, 1)))
            approx = dot(left_rows, stack, ((1,), (0,)))
            decompressed_here[l, at] = approx.astype(bf16)
            errors_here[l, at] = (terms[l, 0, at].astype(f32) + terms[l, 1, at].astype(f32)) - approx
            sem = n if own else len(last_pieces[True]) + n
            send(decompressed_here.at[l, at], decompressed.at[l, at], decompressed_sem.at[sem])
            send(errors_here.at[l, at], new_errors.at[l, at], errors_sem.at[sem])
    for copy in copies:
        copy.wait()


def last(terms, p_terms, p_other, inverse, raw):
    layers, _, rows, cols = terms.shape
    shape = (layers, rows, cols)
    rank = inverse.shape[1]
    pieces = len(last_pieces[True]) + len(last_pieces[False])
    return pl.pallas_call(
        last_kernel,
        in_specs=[whole] * 5,
        out_specs=[pl.BlockSpec(memory_space=pltpu.HBM)] * 3,
        out_shape=[
            pltpu.HBM(shape, bf16),
            pltpu.HBM(shape, f32),
            pltpu.HBM((layers, rank, cols), f32),
        ],
        scratch_shapes=[
            pltpu.VMEM(shape, bf16),
            pltpu.VMEM(shape, f32),
            pltpu.VMEM((layers, rank, cols), f32),
            pltpu.SemaphoreType.DMA((pieces,)),
            pltpu.SemaphoreType.DMA((pieces,)),
            pltpu.SemaphoreType.DMA((layers,)),
        ],
        compiler_params=params,
        name="last",
    )(*[in_vmem(x) for x in (terms, p_terms, p_other, inverse, raw)])


def exchange(x, axis, groups=None):
    return lax.all_to_all(x, axis, 0, 0, axis_index_groups=groups, tiled=True)


def swap(x, partner):
    replicas = lax.axis_size("dp")
    pairs = []
    for device in range(replicas):
        px, py, core = partner(device // 8, device // 2 % 4, device % 2)
        pairs.append((device, (px * 4 + py) * 2 + core))
    return lax.ppermute(x, "dp", pairs)


def swap_cores(x):
    return swap(x, lambda x, y, core: (x, y, 1 - core))


def sum_axis(total, turn, scale):
    near, wrap, far = (
        swap(total, lambda x, y, core, to=to: (x ^ to, y, core) if core == turn else (x, y ^ to, core))
        for to in (1, 3, 2)
    )
    return add([total, near, wrap, far], scale)


def on_device(grads, errors, q_prev):
    replicas, slabs, rank = lax.axis_size("dp"), lax.axis_size("tensor"), q_prev.shape[2]
    terms, merged, other, own = left(grads[:, 0], errors[:, 0], jnp.swapaxes(q_prev, 1, 2))
    total, merged = lax.optimization_barrier((add([own, swap_cores(other)]), merged))
    pair_terms = pair(terms, swap_cores(merged))
    p_t = sum_axis(sum_axis(total, 0, 1.0), 1, 1.0 / replicas)
    raw, gram, p_terms = right(pair_terms, p_t)
    raw, p_other = lax.optimization_barrier((raw, swap_cores(p_t)))
    chips = [[2 * chip + core for chip in range(replicas // 2)] for core in range(2)]
    raw = exchange(raw.reshape(replicas // 2, 8, 128), "dp", chips)
    both = exchange(mix(raw, gram, p_other, slabs), "tensor")
    raw, inverse = unmix(both, replicas, rank, 1.0 / replicas)
    decompressed, new_errors, q_new = last(terms, p_terms, p_other, inverse, exchange(raw, "dp"))
    return decompressed, new_errors[:, None], jnp.swapaxes(q_new, 1, 2)


def solution(mesh):
    placed = (P(None, "dp", "tensor", None), P(None, "dp", "tensor", None), P())
    return jax.shard_map(
        on_device,
        mesh=mesh,
        in_specs=placed,
        out_specs=(P(None, "tensor", None), P(None, "dp", "tensor", None), P()),
        check_vma=False,
    )
```

```python
import jax
import jax.numpy as jnp
from jax import lax
from jax.experimental import pallas as pl
from jax.experimental.pallas import tpu as pltpu
from jax.sharding import PartitionSpec as P

highest = lax.Precision.HIGHEST
f32, bf16 = jnp.float32, jnp.bfloat16
block_rows = 512
ahead = 3
last_pieces = {True: [(0, 256), (256, 512), (512, 1024)], False: [(0, 512), (512, 1024)]}


def halves(x):
    high = x.astype(bf16)
    return high, (x - high.astype(f32)).astype(bf16)


def thirds(x):
    high = x.astype(bf16)
    rest = x - high.astype(f32)
    return high, *halves(rest)


def dot(a, b, contract, precision=None):
    return lax.dot_general(a, b, (contract, ((), ())), precision=precision, preferred_element_type=f32)


def split_dot(small, high, low, contract):
    one, two, three = small
    rows = one.shape[0]
    by_high = dot(jnp.concatenate([one, two, three], 0), high, contract)
    by_low = dot(jnp.concatenate([one, two], 0), low, contract)
    small_terms = by_high[rows : 2 * rows] + by_low[:rows]
    tiny_terms = by_high[2 * rows :] + by_low[rows:]
    return by_high[:rows] + (small_terms + tiny_terms)


def this_core():
    return lax.axis_index("dp") % 2


def in_vmem(x):
    return pltpu.with_memory_space_constraint(x, pltpu.VMEM)


whole = pl.BlockSpec(memory_space=pltpu.VMEM)
params = pltpu.CompilerParams(vmem_limit_bytes=16 * 1024 * 1024)


def in_hbm(x):
    return pltpu.with_memory_space_constraint(x, pltpu.HBM)


def left_kernel(grads, errors, q_t, terms, merged_other, other, own, grads_here, errors_here, q_here, q_sem, grads_sem, errors_sem):
    layers, _, rows, _ = terms.shape
    core = this_core()
    pieces = [(l, b) for l in (1 - core, core) for b in range(rows // block_rows)]

    def fetch(n):
        l, b = pieces[n]
        at = pl.ds(b * block_rows, block_rows)
        return (
            pltpu.make_async_copy(grads.at[l, at], grads_here.at[l, at], grads_sem.at[n]),
            pltpu.make_async_copy(errors.at[l, at], errors_here.at[l, at], errors_sem.at[n]),
        )

    q_copy = pltpu.make_async_copy(q_t, q_here, q_sem)
    q_copy.start()
    for n in range(ahead):
        for copy in fetch(n):
            copy.start()
    q_copy.wait()
    for n, (l, b) in enumerate(pieces):
        for copy in fetch(n):
            copy.wait()
        if n + ahead < len(pieces):
            for copy in fetch(n + ahead):
                copy.start()
        at = pl.ds(b * block_rows, block_rows)
        merged = grads_here[l, at].astype(f32) + errors_here[l, at]
        if n < len(pieces) // 2:
            merged_other[at] = merged
        merged_high, merged_low = halves(merged)
        terms[l, 0, at] = merged_high
        terms[l, 1, at] = merged_low
        term = split_dot(thirds(q_here[l]), merged_high, merged_low, ((1,), (1,)))
        part = other if n < len(pieces) // 2 else own
        for lane in range(block_rows // 128):
            part[b * (block_rows // 128) + lane] = term[:, lane * 128 : (lane + 1) * 128]


def left(grads, errors, q_t):
    layers, rows, cols = grads.shape
    rank = q_t.shape[1]
    pieces = layers * rows // block_rows
    return pl.pallas_call(
        left_kernel,
        in_specs=[pl.BlockSpec(memory_space=pltpu.HBM)] * 3,
        out_specs=[whole] * 4,
        out_shape=[
            pltpu.VMEM((layers, 2, rows, cols), bf16),
            pltpu.VMEM((rows, cols), f32),
            pltpu.VMEM((rows // 128, rank, 128), f32),
            pltpu.VMEM((rows // 128, rank, 128), f32),
        ],
        scratch_shapes=[
            pltpu.VMEM(grads.shape, bf16),
            pltpu.VMEM(grads.shape, f32),
            pltpu.VMEM(q_t.shape, f32),
            pltpu.SemaphoreType.DMA,
            pltpu.SemaphoreType.DMA((pieces,)),
            pltpu.SemaphoreType.DMA((pieces,)),
        ],
        compiler_params=params,
        name="left",
    )(in_hbm(grads), in_hbm(errors), in_hbm(q_t))


def add(terms, scale=1.0):
    def kernel(*refs):
        values = [ref[...] for ref in refs[:-1]]
        while len(values) > 1:
            values = [x + y for x, y in zip(values[::2], values[1::2])]
        refs[-1][...] = values[0] * scale

    return pl.pallas_call(
        kernel,
        in_specs=[whole] * len(terms),
        out_specs=whole,
        out_shape=pltpu.VMEM(terms[0].shape, f32),
        compiler_params=params,
        name="add",
    )(*[in_vmem(term) for term in terms])


def pair(terms, merged):
    _, _, rows, cols = terms.shape

    def kernel(terms, merged, out):
        core = this_core()
        both = (terms[core, 0].astype(f32) + terms[core, 1].astype(f32)) + merged[...]
        out[0], out[1] = halves(both)

    return pl.pallas_call(
        kernel,
        in_specs=[whole] * 2,
        out_specs=whole,
        out_shape=pltpu.VMEM((2, rows, cols), bf16),
        compiler_params=params,
        cost_estimate=pl.CostEstimate(flops=4_000_000, bytes_accessed=6 * 1024 * 1024, transcendentals=0),
        name="pair",
    )(in_vmem(terms), in_vmem(merged))


def stack_terms(one, two):
    return jnp.concatenate([one, two, one, jnp.zeros_like(one)], 0).T


def gram_of(p_t):
    tiles, rank, _ = p_t.shape

    def kernel(p_t, out):
        factor = jnp.concatenate([p_t[at] for at in range(tiles)], 1)
        square = dot(factor, factor, ((1,), (1,)), highest)
        out[...] = jnp.concatenate([square[at : at + 8] for at in range(0, rank, 8)], 1)

    return pl.pallas_call(
        kernel,
        in_specs=[whole],
        out_specs=whole,
        out_shape=pltpu.VMEM((8, 128), f32),
        compiler_params=params,
        name="gram",
    )(in_vmem(p_t))


def right_kernel(pair_terms, p_t, raw, p_terms):
    tiles, rank, _ = p_t.shape
    factor = jnp.concatenate([p_t[at] for at in range(tiles)], 1)
    small = thirds(factor)
    term = split_dot(small, pair_terms[0], pair_terms[1], ((1,), (0,)))
    for at in range(raw.shape[0]):
        raw[at] = term[:, at * 128 : (at + 1) * 128]
    p_terms[...] = stack_terms(*small[:2])


def right(pair_terms, p_t):
    _, rows, cols = pair_terms.shape
    rank = p_t.shape[1]
    return pl.pallas_call(
        right_kernel,
        in_specs=[whole] * 2,
        out_specs=[whole] * 2,
        out_shape=[
            pltpu.VMEM((cols // 128, rank, 128), f32),
            pltpu.VMEM((rows, 4 * rank), bf16),
        ],
        compiler_params=params,
        name="right",
    )(in_vmem(pair_terms), in_vmem(p_t))


def mix(raw, gram, gram_other, copies):
    def kernel(raw, gram, gram_other, out):
        both = jnp.concatenate([jnp.sum(raw[...], axis=0), gram[...], gram_other[...]], 0)
        out[...] = jnp.broadcast_to(both[None], out.shape)

    return pl.pallas_call(
        kernel,
        in_specs=[whole] * 3,
        out_specs=whole,
        out_shape=pltpu.VMEM((copies, 24, 128), f32),
        compiler_params=params,
        name="mix",
    )(in_vmem(raw), in_vmem(gram), in_vmem(gram_other))


def lower_inverses(packed, rank):
    groups = rank // 8
    row = lax.broadcasted_iota(jnp.int32, (8, 128), 0)
    lane = lax.broadcasted_iota(jnp.int32, (8, 128), 1)
    first = (lane // rank) % 2 == 0
    tiles = []
    for g in range(groups):
        squares = [tile[:, g * rank : (g + 1) * rank] for tile in packed]
        unit = (lane % rank == row + 8 * g).astype(f32)
        tiles.append(jnp.concatenate(squares + [unit[:, 2 * rank :]], 1))
    pivots = [jnp.ones((8, 128), f32)] * groups
    for start in range(0, rank, 16):
        columns = {}
        for k in range(start, start + 16):
            for g in range(start // 8, groups):
                columns[k, g] = jnp.where(first, tiles[g][:, k : k + 1], tiles[g][:, rank + k : rank + k + 1])
        for k in range(start, start + 16):
            at, s = divmod(k, 8)
            pivot = columns[k, at][s : s + 1]
            pivots[at] = jnp.where(row == s, pivot, pivots[at])
            over = 1.0 / pivot
            pivot_row = tiles[at][s : s + 1] * over
            entries = {j: columns[j, at][s : s + 1] * over for j in range(k + 1, start + 16)}
            for g in range(at, groups):
                column = columns[k, g]
                if g == at:
                    column = jnp.where(row > s, column, 0.0)
                tiles[g] = tiles[g] - column * pivot_row
                for j, entry in entries.items():
                    columns[j, g] = columns[j, g] - column * entry
    both = jnp.concatenate([tile / jnp.sqrt(pivot) for tile, pivot in zip(tiles, pivots)], 0)
    return [both[:, (2 + l) * rank : (3 + l) * rank] for l in range(2)]


def unmix(x, copies, rank, scale):
    def kernel(x, piece, inverse):
        total = jnp.sum(x[...], axis=0)
        piece[...] = jnp.broadcast_to(total[None, :8] * scale, piece.shape)
        inverse[0], inverse[1] = lower_inverses([total[8:16], total[16:24]], rank)

    return pl.pallas_call(
        kernel,
        in_specs=[whole],
        out_specs=[whole] * 2,
        out_shape=[pltpu.VMEM((copies, 8, 128), f32), pltpu.VMEM((2, rank, rank), f32)],
        compiler_params=params,
        name="unmix",
    )(in_vmem(x))


def last_kernel(
    terms, p_terms, p_other, inverse, raw, decompressed, new_errors, q_new,
    decompressed_here, errors_here, q_here, decompressed_sem, errors_sem, q_sem,
):
    _, _, rows, cols = terms.shape
    rank = inverse.shape[1]
    core = this_core()
    copies = []

    def send(source, target, sem):
        copy = pltpu.make_async_copy(source, target, sem)
        copy.start()
        copies.append(copy)

    for own in (True, False):
        l = core if own else 1 - core
        lower = inverse[0 if own else 1]
        lanes = [[raw[2 * (j * rank // 8 + i) + l] for i in range(rank // 8)] for j in range(cols // 128)]
        sums = jnp.concatenate([jnp.concatenate(tiles, 0) for tiles in lanes], 1)
        q = dot(lower, sums, ((1,), (0,)), highest)
        q_here[l] = q
        send(q_here.at[l], q_new.at[l], q_sem.at[0 if own else 1])
        right_high, right_low = halves(dot(lower, q, ((0,), (0,)), highest))
        stack = jnp.concatenate([right_high, right_high, right_low, jnp.zeros_like(right_high)], 0)
        for n, (start, end) in enumerate(last_pieces[own]):
            at = pl.ds(start, end - start)
            if own:
                left_rows = p_terms[at]
            else:
                tiles = [p_other[tile] for tile in range(start // 128, end // 128)]
                left_rows = stack_terms(*halves(jnp.concatenate(tiles, 1)))
            approx = dot(left_rows, stack, ((1,), (0,)))
            decompressed_here[l, at] = approx.astype(bf16)
            errors_here[l, at] = (terms[l, 0, at].astype(f32) + terms[l, 1, at].astype(f32)) - approx
            sem = n if own else len(last_pieces[True]) + n
            send(decompressed_here.at[l, at], decompressed.at[l, at], decompressed_sem.at[sem])
            send(errors_here.at[l, at], new_errors.at[l, at], errors_sem.at[sem])
    for copy in copies:
        copy.wait()


def last(terms, p_terms, p_other, inverse, raw):
    layers, _, rows, cols = terms.shape
    shape = (layers, rows, cols)
    rank = inverse.shape[1]
    pieces = len(last_pieces[True]) + len(last_pieces[False])
    return pl.pallas_call(
        last_kernel,
        in_specs=[whole] * 5,
        out_specs=[pl.BlockSpec(memory_space=pltpu.HBM)] * 3,
        out_shape=[
            pltpu.HBM(shape, bf16),
            pltpu.HBM(shape, f32),
            pltpu.HBM((layers, rank, cols), f32),
        ],
        scratch_shapes=[
            pltpu.VMEM(shape, bf16),
            pltpu.VMEM(shape, f32),
            pltpu.VMEM((layers, rank, cols), f32),
            pltpu.SemaphoreType.DMA((pieces,)),
            pltpu.SemaphoreType.DMA((pieces,)),
            pltpu.SemaphoreType.DMA((layers,)),
        ],
        compiler_params=params,
        name="last",
    )(*[in_vmem(x) for x in (terms, p_terms, p_other, inverse, raw)])


def exchange(x, axis, groups=None):
    return lax.all_to_all(x, axis, 0, 0, axis_index_groups=groups, tiled=True)


def swap(x, partner):
    replicas = lax.axis_size("dp")
    pairs = []
    for device in range(replicas):
        px, py, core = partner(device // 8, device // 2 % 4, device % 2)
        pairs.append((device, (px * 4 + py) * 2 + core))
    return lax.ppermute(x, "dp", pairs)


def swap_cores(x):
    return swap(x, lambda x, y, core: (x, y, 1 - core))


def sum_axis(total, turn, scale):
    near, wrap, far = (
        swap(total, lambda x, y, core, to=to: (x ^ to, y, core) if core == turn else (x, y ^ to, core))
        for to in (1, 3, 2)
    )
    return add([total, near, wrap, far], scale)


def on_device(grads, errors, q_prev):
    replicas, slabs, rank = lax.axis_size("dp"), lax.axis_size("tensor"), q_prev.shape[2]
    terms, merged, other, own = left(grads[:, 0], errors[:, 0], jnp.swapaxes(q_prev, 1, 2))
    total, merged = lax.optimization_barrier((add([own, swap_cores(other)]), merged))
    pair_terms = pair(terms, swap_cores(merged))
    p_t = sum_axis(sum_axis(total, 0, 1.0), 1, 1.0 / replicas)
    gram = gram_of(p_t)
    raw, p_terms = right(pair_terms, p_t)
    raw, p_other, gram_other = lax.optimization_barrier((raw, swap_cores(p_t), swap_cores(gram)))
    chips = [[2 * chip + core for chip in range(replicas // 2)] for core in range(2)]
    raw = exchange(raw.reshape(replicas // 2, 8, 128), "dp", chips)
    both = exchange(mix(raw, gram, gram_other, slabs), "tensor")
    raw, inverse = unmix(both, replicas, rank, 1.0 / replicas)
    decompressed, new_errors, q_new = last(terms, p_terms, p_other, inverse, exchange(raw, "dp"))
    return decompressed, new_errors[:, None], jnp.swapaxes(q_new, 1, 2)


def solution(mesh):
    placed = (P(None, "dp", "tensor", None), P(None, "dp", "tensor", None), P())
    return jax.shard_map(
        on_device,
        mesh=mesh,
        in_specs=placed,
        out_specs=(P(None, "tensor", None), P(None, "dp", "tensor", None), P()),
        check_vma=False,
    )
```

```python
import jax
import jax.numpy as jnp
from jax import lax
from jax.experimental import pallas as pl
from jax.experimental.pallas import tpu as pltpu
from jax.sharding import PartitionSpec as P

highest = lax.Precision.HIGHEST
f32, bf16 = jnp.float32, jnp.bfloat16
block_rows = 512
ahead = 3
last_pieces = {True: [(0, 256), (256, 512), (512, 1024)], False: [(0, 512), (512, 1024)]}


def halves(x):
    high = x.astype(bf16)
    return high, (x - high.astype(f32)).astype(bf16)


def thirds(x):
    high = x.astype(bf16)
    rest = x - high.astype(f32)
    return high, *halves(rest)


def dot(a, b, contract, precision=None):
    return lax.dot_general(a, b, (contract, ((), ())), precision=precision, preferred_element_type=f32)


def split_dot(small, high, low, contract):
    one, two, three = small
    rows = one.shape[0]
    by_high = dot(jnp.concatenate([one, two, three], 0), high, contract)
    by_low = dot(jnp.concatenate([one, two], 0), low, contract)
    small_terms = by_high[rows : 2 * rows] + by_low[:rows]
    tiny_terms = by_high[2 * rows :] + by_low[rows:]
    return by_high[:rows] + (small_terms + tiny_terms)


def this_core():
    return lax.axis_index("dp") % 2


def in_vmem(x):
    return pltpu.with_memory_space_constraint(x, pltpu.VMEM)


whole = pl.BlockSpec(memory_space=pltpu.VMEM)
params = pltpu.CompilerParams(vmem_limit_bytes=16 * 1024 * 1024)


def in_hbm(x):
    return pltpu.with_memory_space_constraint(x, pltpu.HBM)


def left_kernel(grads, errors, q_t, terms, merged_other, other, own, grads_here, errors_here, q_here, q_sem, grads_sem, errors_sem):
    layers, _, rows, _ = terms.shape
    core = this_core()
    pieces = [(l, b) for l in (1 - core, core) for b in range(rows // block_rows)]

    def fetch(n):
        l, b = pieces[n]
        at = pl.ds(b * block_rows, block_rows)
        return (
            pltpu.make_async_copy(grads.at[l, at], grads_here.at[l, at], grads_sem.at[n]),
            pltpu.make_async_copy(errors.at[l, at], errors_here.at[l, at], errors_sem.at[n]),
        )

    q_copy = pltpu.make_async_copy(q_t, q_here, q_sem)
    for n in range(ahead):
        for copy in fetch(n):
            copy.start()
        if n == 0:
            q_copy.start()
    for n, (l, b) in enumerate(pieces):
        for copy in fetch(n):
            copy.wait()
        if n + ahead < len(pieces):
            for copy in fetch(n + ahead):
                copy.start()
        at = pl.ds(b * block_rows, block_rows)
        merged = grads_here[l, at].astype(f32) + errors_here[l, at]
        if n < len(pieces) // 2:
            merged_other[at] = merged
        merged_high, merged_low = halves(merged)
        terms[l, 0, at] = merged_high
        terms[l, 1, at] = merged_low
        if n == 0:
            q_copy.wait()
        term = split_dot(thirds(q_here[l]), merged_high, merged_low, ((1,), (1,)))
        part = other if n < len(pieces) // 2 else own
        for lane in range(block_rows // 128):
            part[b * (block_rows // 128) + lane] = term[:, lane * 128 : (lane + 1) * 128]


def left(grads, errors, q_t):
    layers, rows, cols = grads.shape
    rank = q_t.shape[1]
    pieces = layers * rows // block_rows
    return pl.pallas_call(
        left_kernel,
        in_specs=[pl.BlockSpec(memory_space=pltpu.HBM)] * 3,
        out_specs=[whole] * 4,
        out_shape=[
            pltpu.VMEM((layers, 2, rows, cols), bf16),
            pltpu.VMEM((rows, cols), f32),
            pltpu.VMEM((rows // 128, rank, 128), f32),
            pltpu.VMEM((rows // 128, rank, 128), f32),
        ],
        scratch_shapes=[
            pltpu.VMEM(grads.shape, bf16),
            pltpu.VMEM(grads.shape, f32),
            pltpu.VMEM(q_t.shape, f32),
            pltpu.SemaphoreType.DMA,
            pltpu.SemaphoreType.DMA((pieces,)),
            pltpu.SemaphoreType.DMA((pieces,)),
        ],
        compiler_params=params,
        name="left",
    )(in_hbm(grads), in_hbm(errors), in_hbm(q_t))


def add(terms, scale=1.0):
    def kernel(*refs):
        values = [ref[...] for ref in refs[:-1]]
        while len(values) > 1:
            values = [x + y for x, y in zip(values[::2], values[1::2])]
        refs[-1][...] = values[0] * scale

    return pl.pallas_call(
        kernel,
        in_specs=[whole] * len(terms),
        out_specs=whole,
        out_shape=pltpu.VMEM(terms[0].shape, f32),
        compiler_params=params,
        name="add",
    )(*[in_vmem(term) for term in terms])


def pair(terms, merged):
    _, _, rows, cols = terms.shape

    def kernel(terms, merged, out):
        core = this_core()
        both = (terms[core, 0].astype(f32) + terms[core, 1].astype(f32)) + merged[...]
        out[0], out[1] = halves(both)

    return pl.pallas_call(
        kernel,
        in_specs=[whole] * 2,
        out_specs=whole,
        out_shape=pltpu.VMEM((2, rows, cols), bf16),
        compiler_params=params,
        cost_estimate=pl.CostEstimate(flops=4_000_000, bytes_accessed=6 * 1024 * 1024, transcendentals=0),
        name="pair",
    )(in_vmem(terms), in_vmem(merged))


def stack_terms(one, two):
    return jnp.concatenate([one, two, one, jnp.zeros_like(one)], 0).T


def packed_gram(factor):
    rank = factor.shape[0]
    square = dot(factor, factor, ((1,), (1,)), highest)
    return jnp.concatenate([square[at : at + 8] for at in range(0, rank, 8)], 1)


def right_kernel(pair_terms, p_t, raw, gram, p_terms):
    tiles, rank, _ = p_t.shape
    factor = jnp.concatenate([p_t[at] for at in range(tiles)], 1)
    small = thirds(factor)
    term = split_dot(small, pair_terms[0], pair_terms[1], ((1,), (0,)))
    for at in range(raw.shape[0]):
        raw[at] = term[:, at * 128 : (at + 1) * 128]
    gram[...] = packed_gram(factor)
    p_terms[...] = stack_terms(*small[:2])


def right(pair_terms, p_t):
    _, rows, cols = pair_terms.shape
    rank = p_t.shape[1]
    return pl.pallas_call(
        right_kernel,
        in_specs=[whole] * 2,
        out_specs=[whole] * 3,
        out_shape=[
            pltpu.VMEM((cols // 128, rank, 128), f32),
            pltpu.VMEM((8, 128), f32),
            pltpu.VMEM((rows, 4 * rank), bf16),
        ],
        compiler_params=params,
        name="right",
    )(in_vmem(pair_terms), in_vmem(p_t))


def mix(raw, gram, p_other, copies):
    def kernel(raw, gram, p_other, out):
        factor = jnp.concatenate([p_other[at] for at in range(p_other.shape[0])], 1)
        both = jnp.concatenate([jnp.sum(raw[...], axis=0), gram[...], packed_gram(factor)], 0)
        out[...] = jnp.broadcast_to(both[None], out.shape)

    return pl.pallas_call(
        kernel,
        in_specs=[whole] * 3,
        out_specs=whole,
        out_shape=pltpu.VMEM((copies, 24, 128), f32),
        compiler_params=params,
        name="mix",
    )(in_vmem(raw), in_vmem(gram), in_vmem(p_other))


def lower_inverses(packed, rank):
    groups = rank // 8
    row = lax.broadcasted_iota(jnp.int32, (8, 128), 0)
    lane = lax.broadcasted_iota(jnp.int32, (8, 128), 1)
    first = (lane // rank) % 2 == 0
    tiles = []
    for g in range(groups):
        squares = [tile[:, g * rank : (g + 1) * rank] for tile in packed]
        unit = (lane % rank == row + 8 * g).astype(f32)
        tiles.append(jnp.concatenate(squares + [unit[:, 2 * rank :]], 1))
    pivots = [jnp.ones((8, 128), f32)] * groups
    for start in range(0, rank, 16):
        columns = {}
        for k in range(start, start + 16):
            for g in range(start // 8, groups):
                columns[k, g] = jnp.where(first, tiles[g][:, k : k + 1], tiles[g][:, rank + k : rank + k + 1])
        for k in range(start, start + 16):
            at, s = divmod(k, 8)
            pivot = columns[k, at][s : s + 1]
            pivots[at] = jnp.where(row == s, pivot, pivots[at])
            over = 1.0 / pivot
            pivot_row = tiles[at][s : s + 1] * over
            entries = {j: columns[j, at][s : s + 1] * over for j in range(k + 1, start + 16)}
            for g in range(at, groups):
                column = columns[k, g]
                if g == at:
                    column = jnp.where(row > s, column, 0.0)
                tiles[g] = tiles[g] - column * pivot_row
                for j, entry in entries.items():
                    columns[j, g] = columns[j, g] - column * entry
    both = jnp.concatenate([tile / jnp.sqrt(pivot) for tile, pivot in zip(tiles, pivots)], 0)
    return [both[:, (2 + l) * rank : (3 + l) * rank] for l in range(2)]


def unmix(x, copies, rank, scale):
    def kernel(x, piece, inverse):
        total = jnp.sum(x[...], axis=0)
        piece[...] = jnp.broadcast_to(total[None, :8] * scale, piece.shape)
        inverse[0], inverse[1] = lower_inverses([total[8:16], total[16:24]], rank)

    return pl.pallas_call(
        kernel,
        in_specs=[whole],
        out_specs=[whole] * 2,
        out_shape=[pltpu.VMEM((copies, 8, 128), f32), pltpu.VMEM((2, rank, rank), f32)],
        compiler_params=params,
        name="unmix",
    )(in_vmem(x))


def last_kernel(
    terms, p_terms, p_other, inverse, raw, decompressed, new_errors, q_new,
    decompressed_here, errors_here, q_here, decompressed_sem, errors_sem, q_sem,
):
    _, _, rows, cols = terms.shape
    rank = inverse.shape[1]
    core = this_core()
    copies = []

    def send(source, target, sem):
        copy = pltpu.make_async_copy(source, target, sem)
        copy.start()
        copies.append(copy)

    for own in (True, False):
        l = core if own else 1 - core
        lower = inverse[0 if own else 1]
        lanes = [[raw[2 * (j * rank // 8 + i) + l] for i in range(rank // 8)] for j in range(cols // 128)]
        sums = jnp.concatenate([jnp.concatenate(tiles, 0) for tiles in lanes], 1)
        q = dot(lower, sums, ((1,), (0,)), highest)
        q_here[l] = q
        send(q_here.at[l], q_new.at[l], q_sem.at[0 if own else 1])
        right_high, right_low = halves(dot(lower, q, ((0,), (0,)), highest))
        stack = jnp.concatenate([right_high, right_high, right_low, jnp.zeros_like(right_high)], 0)
        for n, (start, end) in enumerate(last_pieces[own]):
            at = pl.ds(start, end - start)
            if own:
                left_rows = p_terms[at]
            else:
                tiles = [p_other[tile] for tile in range(start // 128, end // 128)]
                left_rows = stack_terms(*halves(jnp.concatenate(tiles, 1)))
            approx = dot(left_rows, stack, ((1,), (0,)))
            decompressed_here[l, at] = approx.astype(bf16)
            errors_here[l, at] = (terms[l, 0, at].astype(f32) + terms[l, 1, at].astype(f32)) - approx
            sem = n if own else len(last_pieces[True]) + n
            send(decompressed_here.at[l, at], decompressed.at[l, at], decompressed_sem.at[sem])
            send(errors_here.at[l, at], new_errors.at[l, at], errors_sem.at[sem])
    for copy in copies:
        copy.wait()


def last(terms, p_terms, p_other, inverse, raw):
    layers, _, rows, cols = terms.shape
    shape = (layers, rows, cols)
    rank = inverse.shape[1]
    pieces = len(last_pieces[True]) + len(last_pieces[False])
    return pl.pallas_call(
        last_kernel,
        in_specs=[whole] * 5,
        out_specs=[pl.BlockSpec(memory_space=pltpu.HBM)] * 3,
        out_shape=[
            pltpu.HBM(shape, bf16),
            pltpu.HBM(shape, f32),
            pltpu.HBM((layers, rank, cols), f32),
        ],
        scratch_shapes=[
            pltpu.VMEM(shape, bf16),
            pltpu.VMEM(shape, f32),
            pltpu.VMEM((layers, rank, cols), f32),
            pltpu.SemaphoreType.DMA((pieces,)),
            pltpu.SemaphoreType.DMA((pieces,)),
            pltpu.SemaphoreType.DMA((layers,)),
        ],
        compiler_params=params,
        name="last",
    )(*[in_vmem(x) for x in (terms, p_terms, p_other, inverse, raw)])


def exchange(x, axis, groups=None):
    return lax.all_to_all(x, axis, 0, 0, axis_index_groups=groups, tiled=True)


def swap(x, partner):
    replicas = lax.axis_size("dp")
    pairs = []
    for device in range(replicas):
        px, py, core = partner(device // 8, device // 2 % 4, device % 2)
        pairs.append((device, (px * 4 + py) * 2 + core))
    return lax.ppermute(x, "dp", pairs)


def swap_cores(x):
    return swap(x, lambda x, y, core: (x, y, 1 - core))


def sum_axis(total, turn, scale):
    near, wrap, far = (
        swap(total, lambda x, y, core, to=to: (x ^ to, y, core) if core == turn else (x, y ^ to, core))
        for to in (1, 3, 2)
    )
    return add([total, near, wrap, far], scale)


def on_device(grads, errors, q_prev):
    replicas, slabs, rank = lax.axis_size("dp"), lax.axis_size("tensor"), q_prev.shape[2]
    terms, merged, other, own = left(grads[:, 0], errors[:, 0], jnp.swapaxes(q_prev, 1, 2))
    total, merged = lax.optimization_barrier((add([own, swap_cores(other)]), merged))
    pair_terms = pair(terms, swap_cores(merged))
    p_t = sum_axis(sum_axis(total, 0, 1.0), 1, 1.0 / replicas)
    raw, gram, p_terms = right(pair_terms, p_t)
    raw, p_other = lax.optimization_barrier((raw, swap_cores(p_t)))
    chips = [[2 * chip + core for chip in range(replicas // 2)] for core in range(2)]
    raw = exchange(raw.reshape(replicas // 2, 8, 128), "dp", chips)
    both = exchange(mix(raw, gram, p_other, slabs), "tensor")
    raw, inverse = unmix(both, replicas, rank, 1.0 / replicas)
    decompressed, new_errors, q_new = last(terms, p_terms, p_other, inverse, exchange(raw, "dp"))
    return decompressed, new_errors[:, None], jnp.swapaxes(q_new, 1, 2)


def solution(mesh):
    placed = (P(None, "dp", "tensor", None), P(None, "dp", "tensor", None), P())
    return jax.shard_map(
        on_device,
        mesh=mesh,
        in_specs=placed,
        out_specs=(P(None, "tensor", None), P(None, "dp", "tensor", None), P()),
        check_vma=False,
    )
```

```python
import jax
import jax.numpy as jnp
from jax import lax
from jax.experimental import pallas as pl
from jax.experimental.pallas import tpu as pltpu
from jax.sharding import PartitionSpec as P

highest = lax.Precision.HIGHEST
f32, bf16 = jnp.float32, jnp.bfloat16
block_rows = 512
ahead = 3
last_pieces = {True: [(0, 256), (256, 512), (512, 1024)], False: [(0, 512), (512, 1024)]}


def halves(x):
    high = x.astype(bf16)
    return high, (x - high.astype(f32)).astype(bf16)


def thirds(x):
    high = x.astype(bf16)
    rest = x - high.astype(f32)
    return high, *halves(rest)


def dot(a, b, contract, precision=None):
    return lax.dot_general(a, b, (contract, ((), ())), precision=precision, preferred_element_type=f32)


def split_dot(small, high, low, contract):
    one, two, three = small
    rows = one.shape[0]
    by_high = dot(jnp.concatenate([one, two, three], 0), high, contract)
    by_low = dot(jnp.concatenate([one, two], 0), low, contract)
    small_terms = by_high[rows : 2 * rows] + by_low[:rows]
    tiny_terms = by_high[2 * rows :] + by_low[rows:]
    return by_high[:rows] + (small_terms + tiny_terms)


def this_core():
    return lax.axis_index("dp") % 2


def in_vmem(x):
    return pltpu.with_memory_space_constraint(x, pltpu.VMEM)


whole = pl.BlockSpec(memory_space=pltpu.VMEM)
params = pltpu.CompilerParams(vmem_limit_bytes=16 * 1024 * 1024)


def in_hbm(x):
    return pltpu.with_memory_space_constraint(x, pltpu.HBM)


def left_kernel(grads, errors, q_t, terms, merged_other, other, own, grads_here, errors_here, q_here, q_sem, grads_sem, errors_sem):
    layers, _, rows, _ = terms.shape
    core = this_core()
    pieces = [(l, b) for l in (1 - core, core) for b in range(rows // block_rows)]

    def fetch(n):
        l, b = pieces[n]
        at = pl.ds(b * block_rows, block_rows)
        return (
            pltpu.make_async_copy(grads.at[l, at], grads_here.at[l, at], grads_sem.at[n]),
            pltpu.make_async_copy(errors.at[l, at], errors_here.at[l, at], errors_sem.at[n]),
        )

    q_copy = pltpu.make_async_copy(q_t, q_here, q_sem)
    q_copy.start()
    for n in range(ahead):
        for copy in fetch(n):
            copy.start()
    q_copy.wait()
    for n, (l, b) in enumerate(pieces):
        for copy in fetch(n):
            copy.wait()
        if n + ahead < len(pieces):
            for copy in fetch(n + ahead):
                copy.start()
        at = pl.ds(b * block_rows, block_rows)
        merged = grads_here[l, at].astype(f32) + errors_here[l, at]
        if n < len(pieces) // 2:
            merged_other[at] = merged
        merged_high, merged_low = halves(merged)
        terms[l, 0, at] = merged_high
        terms[l, 1, at] = merged_low
        term = split_dot(thirds(q_here[l]), merged_high, merged_low, ((1,), (1,)))
        part = other if n < len(pieces) // 2 else own
        for lane in range(block_rows // 128):
            part[b * (block_rows // 128) + lane] = term[:, lane * 128 : (lane + 1) * 128]


def left(grads, errors, q_t):
    layers, rows, cols = grads.shape
    rank = q_t.shape[1]
    pieces = layers * rows // block_rows
    return pl.pallas_call(
        left_kernel,
        in_specs=[pl.BlockSpec(memory_space=pltpu.HBM)] * 3,
        out_specs=[whole] * 4,
        out_shape=[
            pltpu.VMEM((layers, 2, rows, cols), bf16),
            pltpu.VMEM((rows, cols), f32),
            pltpu.VMEM((rows // 128, rank, 128), f32),
            pltpu.VMEM((rows // 128, rank, 128), f32),
        ],
        scratch_shapes=[
            pltpu.VMEM(grads.shape, bf16),
            pltpu.VMEM(grads.shape, f32),
            pltpu.VMEM(q_t.shape, f32),
            pltpu.SemaphoreType.DMA,
            pltpu.SemaphoreType.DMA((pieces,)),
            pltpu.SemaphoreType.DMA((pieces,)),
        ],
        compiler_params=params,
        name="left",
    )(in_hbm(grads), in_hbm(errors), in_hbm(q_t))


def add(terms, scale=1.0):
    def kernel(*refs):
        values = [ref[...] for ref in refs[:-1]]
        while len(values) > 1:
            values = [x + y for x, y in zip(values[::2], values[1::2])]
        refs[-1][...] = values[0] * scale

    return pl.pallas_call(
        kernel,
        in_specs=[whole] * len(terms),
        out_specs=whole,
        out_shape=pltpu.VMEM(terms[0].shape, f32),
        compiler_params=params,
        name="add",
    )(*[in_vmem(term) for term in terms])


def pair(terms, merged):
    _, _, rows, cols = terms.shape

    def kernel(terms, merged, out):
        core = this_core()
        both = (terms[core, 0].astype(f32) + terms[core, 1].astype(f32)) + merged[...]
        out[0], out[1] = halves(both)

    return pl.pallas_call(
        kernel,
        in_specs=[whole] * 2,
        out_specs=whole,
        out_shape=pltpu.VMEM((2, rows, cols), bf16),
        compiler_params=params,
        cost_estimate=pl.CostEstimate(flops=4_000_000, bytes_accessed=6 * 1024 * 1024, transcendentals=0),
        name="pair",
    )(in_vmem(terms), in_vmem(merged))


def stack_terms(one, two):
    return jnp.concatenate([one, two, one, jnp.zeros_like(one)], 0).T


def packed_gram(factor):
    rank = factor.shape[0]
    square = dot(factor, factor, ((1,), (1,)), highest)
    return jnp.concatenate([square[at : at + 8] for at in range(0, rank, 8)], 1)


def right_kernel(pair_terms, p_t, raw, gram, p_terms):
    tiles, rank, _ = p_t.shape
    factor = jnp.concatenate([p_t[at] for at in range(tiles)], 1)
    small = thirds(factor)
    term = split_dot(small, pair_terms[0], pair_terms[1], ((1,), (0,)))
    for at in range(raw.shape[0]):
        raw[at] = term[:, at * 128 : (at + 1) * 128]
    gram[...] = packed_gram(factor)
    p_terms[...] = stack_terms(*small[:2])


def right(pair_terms, p_t):
    _, rows, cols = pair_terms.shape
    rank = p_t.shape[1]
    return pl.pallas_call(
        right_kernel,
        in_specs=[whole] * 2,
        out_specs=[whole] * 3,
        out_shape=[
            pltpu.VMEM((cols // 128, rank, 128), f32),
            pltpu.VMEM((8, 128), f32),
            pltpu.VMEM((rows, 4 * rank), bf16),
        ],
        compiler_params=params,
        name="right",
    )(in_vmem(pair_terms), in_vmem(p_t))


def mix(raw, gram, p_other, copies):
    def kernel(raw, gram, p_other, out):
        factor = jnp.concatenate([p_other[at] for at in range(p_other.shape[0])], 1)
        both = jnp.concatenate([jnp.sum(raw[...], axis=0), gram[...], packed_gram(factor)], 0)
        out[...] = jnp.broadcast_to(both[None], out.shape)

    return pl.pallas_call(
        kernel,
        in_specs=[whole] * 3,
        out_specs=whole,
        out_shape=pltpu.VMEM((copies, 24, 128), f32),
        compiler_params=params,
        name="mix",
    )(in_vmem(raw), in_vmem(gram), in_vmem(p_other))


def lower_inverses(packed, rank):
    groups = rank // 8
    row = lax.broadcasted_iota(jnp.int32, (8, 128), 0)
    lane = lax.broadcasted_iota(jnp.int32, (8, 128), 1)
    first = (lane // rank) % 2 == 0
    tiles = []
    for g in range(groups):
        squares = [tile[:, g * rank : (g + 1) * rank] for tile in packed]
        unit = (lane % rank == row + 8 * g).astype(f32)
        tiles.append(jnp.concatenate(squares + [unit[:, 2 * rank :]], 1))
    pivots = [jnp.ones((8, 128), f32)] * groups
    for start in range(0, rank, 16):
        columns = {}
        for k in range(start, start + 16):
            for g in range(start // 8, groups):
                columns[k, g] = jnp.where(first, tiles[g][:, k : k + 1], tiles[g][:, rank + k : rank + k + 1])
        for k in range(start, start + 16):
            at, s = divmod(k, 8)
            pivot = columns[k, at][s : s + 1]
            pivots[at] = jnp.where(row == s, pivot, pivots[at])
            over = 1.0 / pivot
            pivot_row = tiles[at][s : s + 1] * over
            entries = {j: columns[j, at][s : s + 1] * over for j in range(k + 1, start + 16)}
            for g in range(at, groups):
                column = columns[k, g]
                if g == at:
                    column = jnp.where(row > s, column, 0.0)
                tiles[g] = tiles[g] - column * pivot_row
                for j, entry in entries.items():
                    columns[j, g] = columns[j, g] - column * entry
    both = jnp.concatenate([tile / jnp.sqrt(pivot) for tile, pivot in zip(tiles, pivots)], 0)
    return [both[:, (2 + l) * rank : (3 + l) * rank] for l in range(2)]


def unmix(x, copies, rank, scale):
    def kernel(x, piece, inverse):
        total = jnp.sum(x[...], axis=0)
        piece[...] = jnp.broadcast_to(total[None, :8] * scale, piece.shape)
        inverse[0], inverse[1] = lower_inverses([total[8:16], total[16:24]], rank)

    return pl.pallas_call(
        kernel,
        in_specs=[whole],
        out_specs=[whole] * 2,
        out_shape=[pltpu.VMEM((copies, 8, 128), f32), pltpu.VMEM((2, rank, rank), f32)],
        compiler_params=params,
        name="unmix",
    )(in_vmem(x))


def last_kernel(
    terms, p_terms, p_other, inverse, raw, decompressed, new_errors, q_new,
    decompressed_here, errors_here, q_here, decompressed_sem, errors_sem, q_sem,
):
    _, _, rows, cols = terms.shape
    rank = inverse.shape[1]
    core = this_core()
    copies = []

    def send(source, target, sem):
        copy = pltpu.make_async_copy(source, target, sem)
        copy.start()
        copies.append(copy)

    for own in (True, False):
        l = core if own else 1 - core
        lower = inverse[0 if own else 1]
        lanes = [[raw[2 * (j * rank // 8 + i) + l] for i in range(rank // 8)] for j in range(cols // 128)]
        sums = jnp.concatenate([jnp.concatenate(tiles, 0) for tiles in lanes], 1)
        q = dot(lower, sums, ((1,), (0,)), highest)
        q_here[l] = q
        send(q_here.at[l], q_new.at[l], q_sem.at[0 if own else 1])
        right_high, right_low = halves(dot(lower, q, ((0,), (0,)), highest))
        stack = jnp.concatenate([right_high, right_high, right_low, jnp.zeros_like(right_high)], 0)
        for n, (start, end) in enumerate(last_pieces[own]):
            at = pl.ds(start, end - start)
            if own:
                left_rows = p_terms[at]
            else:
                tiles = [p_other[tile] for tile in range(start // 128, end // 128)]
                left_rows = stack_terms(*halves(jnp.concatenate(tiles, 1)))
            approx = dot(left_rows, stack, ((1,), (0,)))
            decompressed_here[l, at] = approx.astype(bf16)
            errors_here[l, at] = (terms[l, 0, at].astype(f32) + terms[l, 1, at].astype(f32)) - approx
            sem = n if own else len(last_pieces[True]) + n
            send(decompressed_here.at[l, at], decompressed.at[l, at], decompressed_sem.at[sem])
            send(errors_here.at[l, at], new_errors.at[l, at], errors_sem.at[sem])
    for copy in copies:
        copy.wait()


def last(terms, p_terms, p_other, inverse, raw):
    layers, _, rows, cols = terms.shape
    shape = (layers, rows, cols)
    rank = inverse.shape[1]
    pieces = len(last_pieces[True]) + len(last_pieces[False])
    return pl.pallas_call(
        last_kernel,
        in_specs=[whole] * 5,
        out_specs=[pl.BlockSpec(memory_space=pltpu.HBM)] * 3,
        out_shape=[
            pltpu.HBM(shape, bf16),
            pltpu.HBM(shape, f32),
            pltpu.HBM((layers, rank, cols), f32),
        ],
        scratch_shapes=[
            pltpu.VMEM(shape, bf16),
            pltpu.VMEM(shape, f32),
            pltpu.VMEM((layers, rank, cols), f32),
            pltpu.SemaphoreType.DMA((pieces,)),
            pltpu.SemaphoreType.DMA((pieces,)),
            pltpu.SemaphoreType.DMA((layers,)),
        ],
        compiler_params=params,
        name="last",
    )(*[in_vmem(x) for x in (terms, p_terms, p_other, inverse, raw)])


def exchange(x, axis, groups=None):
    return lax.all_to_all(x, axis, 0, 0, axis_index_groups=groups, tiled=True)


def swap(x, partner):
    replicas = lax.axis_size("dp")
    pairs = []
    for device in range(replicas):
        px, py, core = partner(device // 8, device // 2 % 4, device % 2)
        pairs.append((device, (px * 4 + py) * 2 + core))
    return lax.ppermute(x, "dp", pairs)


def swap_cores(x):
    return swap(x, lambda x, y, core: (x, y, 1 - core))


def sum_axis(total, turn, scale):
    near, wrap, far = (
        swap(total, lambda x, y, core, to=to: (x ^ to, y, core) if core != turn else (x, y ^ to, core))
        for to in (1, 3, 2)
    )
    return add([total, near, wrap, far], scale)


def on_device(grads, errors, q_prev):
    replicas, slabs, rank = lax.axis_size("dp"), lax.axis_size("tensor"), q_prev.shape[2]
    terms, merged, other, own = left(grads[:, 0], errors[:, 0], jnp.swapaxes(q_prev, 1, 2))
    total, merged = lax.optimization_barrier((add([own, swap_cores(other)]), merged))
    pair_terms = pair(terms, swap_cores(merged))
    p_t = sum_axis(sum_axis(total, 0, 1.0), 1, 1.0 / replicas)
    raw, gram, p_terms = right(pair_terms, p_t)
    raw, p_other = lax.optimization_barrier((raw, swap_cores(p_t)))
    chips = [[2 * chip + core for chip in range(replicas // 2)] for core in range(2)]
    raw = exchange(raw.reshape(replicas // 2, 8, 128), "dp", chips)
    both = exchange(mix(raw, gram, p_other, slabs), "tensor")
    raw, inverse = unmix(both, replicas, rank, 1.0 / replicas)
    decompressed, new_errors, q_new = last(terms, p_terms, p_other, inverse, exchange(raw, "dp"))
    return decompressed, new_errors[:, None], jnp.swapaxes(q_new, 1, 2)


def solution(mesh):
    placed = (P(None, "dp", "tensor", None), P(None, "dp", "tensor", None), P())
    return jax.shard_map(
        on_device,
        mesh=mesh,
        in_specs=placed,
        out_specs=(P(None, "tensor", None), P(None, "dp", "tensor", None), P()),
        check_vma=False,
    )
```
